256 devices in a mesh: tm: 128 (over x, z, y_hi, core), space: 2 (over y_lo).
Axes of the slice: x: 4, y: 4 (y_hi: 2, y_lo: 2; y = y_hi * 2 + y_lo), z: 8, core: 2. Of those that a mesh axis runs over, the one named last changes fastest.
Arguments:
- guess_states: float32 [128, 8, 8192], P('tm', None, 'space'), may hold values from -6 to 6
- coarse_rate: float32 [128, 8192], P('tm', 'space')
- source: float32 [8192], P('space'), may hold values from -6 to 6
- reaction_rate: float32 [8], replicated, may hold values from 0.5 to 4
- inverse_blocks: float32 [64, 128, 128], P('space'), may hold values from -0.05 to 1
- coupling_blocks: float32 [128, 128, 128], P('space'), may hold values from -0.05 to 0.05
- column_index: int32 [2, 64], P('space'), may hold values from 0 to 33, as said below
- row_offsets: int32 [2, 33], P('space'), may hold values from 0 to 64, as said below
Outputs:
- end_states: float32 [128, 8, 8192], P('tm', None, 'space')
The draws below stay inside these ranges and needn't reach their ends.
Inputs may be any that keep to these rules, and one draw needn't show every extreme that they name: `row_offsets`: each slab's offsets start at 0, rise by 1 to 3 from one block row to the next, every aligned pair of block rows holds four stored blocks together, and the last offset is 64. `column_index`: position 0 is the previous slab's last block and 33 the next slab's first block; a row's stored blocks are distinct, never on its own diagonal, and within two blocks of it; the first block row always couples to position 0 and the last to 33.
All inputs are finite; a program needn't handle non-finite values.
Results may differ from the reference program's by a relative error of at most 0.0003.
Values sent between devices are 32-bit elements; how exact they have to be, the bound alone decides.
No kernel may reach another device: no remote copies, remote signals or barrier semaphores. Data moves between devices by JAX's collectives and lax.ppermute only.
A program may use at most 192 MiB of HBM per device.

```python
import math
import jax
import jax.numpy as jnp
from jax import lax

S = 8
BLK = 128
M = 8
SWEEPS = 2
COARSE_SLICES = 128
TOTAL_CELLS = 8192
NB = 32
NNZ = 64
NBT = 64
NNZT = 128
N_SPACE = 2


def sparsity(key):

    def single_slab(slab_index):
        slab_key = jax.random.fold_in(jax.random.fold_in(key, 17), slab_index)
        key_pattern, key_near, key_far = jax.random.split(slab_key, 3)
        pattern = jax.random.randint(key_pattern, (NB // 2,), 0, 3)
        leading_count = jnp.where(pattern == 0, 1, jnp.where(pattern == 1, 3, 2))
        counts = jnp.stack([leading_count, 4 - leading_count], axis=1).reshape(NB)
        offsets = jnp.concatenate([jnp.zeros((1,), jnp.int32), jnp.cumsum(counts).astype(jnp.int32)])
        row_index = jnp.arange(NB, dtype=jnp.int32)
        near_sign = 2 * jax.random.randint(key_near, (NB,), 0, 2) - 1
        nearest = jnp.where(row_index == 0, -1, jnp.where(row_index == NB - 1, 1, near_sign))
        far_sign = 2 * jax.random.randint(key_far, (NB,), 0, 2) - 1
        farther = jnp.where(row_index == 0, 2, jnp.where(row_index == NB - 1, -2, 2 * far_sign))
        candidates = jnp.stack([nearest, -nearest, farther], axis=1) + row_index[:, None] + 1
        stored = jnp.arange(NNZ, dtype=jnp.int32)
        row_owner = jnp.sum((offsets[None, 1:] <= stored[:, None]).astype(jnp.int32), axis=1)
        slot_index = stored - offsets[row_owner]
        chosen = jnp.take_along_axis(candidates[row_owner], slot_index[:, None], axis=1)[:, 0]
        return (offsets.astype(jnp.int32), chosen.astype(jnp.int32))
    return jax.vmap(single_slab)(jnp.arange(N_SPACE, dtype=jnp.int32))


def draw_row_offsets(key, part):
    return sparsity(key)[0]


def draw_column_index(key, part):
    return sparsity(key)[1]


def draw_coarse_rate(key, part):
    baseline_key, multiplier_key, location_key, spike_key = jax.random.split(jax.random.fold_in(key, 29), 4)
    lower = math.log(0.15 / COARSE_SLICES)
    upper = math.log(0.08)
    baseline_rate = jnp.exp(jax.random.uniform(baseline_key, (1, TOTAL_CELLS), jnp.float32, lower, upper))
    multiplier = jax.random.uniform(multiplier_key, (COARSE_SLICES, TOTAL_CELLS), jnp.float32, 0.6, 1.4)
    locations = jax.random.randint(location_key, (3,), 0, COARSE_SLICES)
    spike_present = jnp.any(jnp.arange(COARSE_SLICES)[:, None] == locations[None, :], axis=1)
    spike_amplitude = jax.random.uniform(spike_key, (COARSE_SLICES, TOTAL_CELLS), jnp.float32, 0.25, 0.7)
    return baseline_rate * multiplier + jnp.where(spike_present[:, None], spike_amplitude, 0.0)


def draw_source(key, part):
    key_rough = jax.random.fold_in(key, 41)
    return jnp.clip(jax.random.normal(key_rough, (TOTAL_CELLS,), jnp.float32), -6.0, 6.0)


def draw_inverse_blocks(key, part):
    key_diagonal, key_noise = jax.random.split(jax.random.fold_in(key, 53), 2)
    identity = jnp.eye(BLK, dtype=jnp.float32)
    diagonal = jax.random.uniform(key_diagonal, (NBT, BLK, 1), jnp.float32, 0.7, 0.95)
    noise = jnp.clip(0.003 * jax.random.normal(key_noise, (NBT, BLK, BLK), jnp.float32), -0.02, 0.02)
    return noise * (1.0 - identity) + identity * diagonal


def level_of(own_key, shape, cuts, low, high):
    def one(position, parts):
        steps = jax.random.uniform(jax.random.fold_in(jax.random.fold_in(own_key, 6), position), (parts,), jnp.float32, low / len(cuts), high / len(cuts))
        return jnp.repeat(jnp.exp(steps), shape[position] // parts).reshape((-1,) + (1,) * (len(shape) - position - 1))

    gain = one(*cuts[0])
    for cut in cuts[1:]:
        gain = gain * one(*cut)
    return gain


def bell_draw(key, dims, spread, most, cuts=(), held_as=jnp.bfloat16):
    factor_of = level_of(key, dims, cuts, -0.22, 0.18) if cuts else 1.0
    array = jax.random.normal(key, dims, jnp.float32) * spread * factor_of
    return jnp.minimum(jnp.maximum(array, -most), most).astype(held_as)


def setup_inputs(seed: int = 0) -> dict:
    key_of = jax.random.split(jax.random.key(seed), 9)
    return {
        "guess_states": bell_draw(key_of[0], (COARSE_SLICES, S, TOTAL_CELLS), 1.0, 6.0, ((0, 128), (2, 2)), jnp.float32),
        "coarse_rate": draw_coarse_rate(jax.random.fold_in(key_of[8], 71), 0),
        "source": draw_source(jax.random.fold_in(key_of[8], 71), 0),
        "reaction_rate": jnp.clip(jnp.exp(jax.random.uniform(key_of[3], (S,), jnp.float32, math.log(0.5), math.log(4.0))), 0.5, 4.0),
        "inverse_blocks": draw_inverse_blocks(jax.random.fold_in(key_of[8], 71), 0),
        "coupling_blocks": bell_draw(key_of[5], (NNZT, BLK, BLK), 0.008, 0.05, ((0, 2),), jnp.float32),
        "column_index": draw_column_index(jax.random.fold_in(key_of[8], 71), 0),
        "row_offsets": draw_row_offsets(jax.random.fold_in(key_of[8], 71), 0),
    }


step_size = 0.25


def fine_step(current, source, reaction_rate, inverse_blocks, coupling_blocks, columns, row_owner):
    scenarios = current.shape[0]
    block_count = inverse_blocks.shape[0]
    block_size = inverse_blocks.shape[1]
    right_side = current + step_size * (source[None, :] - reaction_rate[:, None] * jnp.tanh(current))

    def invert(vector):
        blocked = vector.reshape(scenarios, block_count, block_size)
        applied = jnp.einsum("nik,snk->sni", inverse_blocks, blocked, precision=lax.Precision.HIGHEST)
        return applied.reshape(scenarios, block_count * block_size)

    def couple(vector):
        blocked = vector.reshape(scenarios, block_count, block_size)
        margin = jnp.zeros((scenarios, 1, block_size), jnp.float32)
        padded = jnp.concatenate([margin, blocked, margin], axis=1)
        picked = jnp.take(padded, columns, axis=1)
        products = jnp.einsum("jik,sjk->sji", coupling_blocks, picked, precision=lax.Precision.HIGHEST)
        summed = jax.ops.segment_sum(jnp.transpose(products, (1, 0, 2)), row_owner, num_segments=block_count)
        return jnp.transpose(summed, (1, 0, 2)).reshape(scenarios, block_count * block_size)

    iterate = invert(right_side)
    for sweep_index in range(SWEEPS):
        iterate = invert(right_side - couple(iterate))
    return iterate


def reference(guess_states, coarse_rate, source, reaction_rate, inverse_blocks, coupling_blocks, column_index, row_offsets):
    slab_index = jnp.arange(N_SPACE, dtype=jnp.int32)[:, None]
    columns = (column_index + slab_index * NB).reshape(-1).astype(jnp.int32)
    stored = jnp.arange(NNZ, dtype=jnp.int32)
    owners = jnp.sum((row_offsets[:, 1:, None] <= stored[None, None, :]).astype(jnp.int32), axis=1)
    row_owner = (owners + slab_index * NB).reshape(-1).astype(jnp.int32)

    def propagate(current):
        for step_index in range(M):
            current = fine_step(current, source, reaction_rate, inverse_blocks, coupling_blocks, columns, row_owner)
        return current

    advanced = lax.map(propagate, guess_states)
    relaxed = jnp.concatenate([guess_states[:1], advanced[:-1]], axis=0)
    settled = lax.map(propagate, relaxed)
    coarse_decay = 1.0 / (1.0 + coarse_rate)
    residual = settled[:-1] - relaxed[1:]

    def chained(carried, inputs):
        multiplier, term = inputs
        carried = multiplier[None, :] * carried + term
        return carried, carried

    starting = jnp.zeros(guess_states.shape[1:], jnp.float32)
    unused, later_errors = lax.scan(chained, starting, (coarse_decay[:-1], residual))
    errors = jnp.concatenate([starting[None], later_errors], axis=0)
    return settled + coarse_decay[:, None, :] * errors
```

```python
import functools

import jax
import jax.numpy as jnp
from jax import lax
from jax.experimental import pallas as pl
from jax.experimental.pallas import tpu as pltpu
from jax.sharding import PartitionSpec as P

M = 8
SWEEPS = 2
STEPS = 2
ROUNDS = 2 * M // STEPS
NB = 32
PAIRS = NB // 2
GROWS = 4 * STEPS
GPAIRS = GROWS // 2 - 1
WIN = NB + GROWS + 1
S = 8
BLK = 128
LOW = NB - GROWS

step_size = 0.25

bf16 = jnp.bfloat16
f32 = jnp.float32


def halves(value):
    high = value.astype(bf16)
    return high, (value - high.astype(f32)).astype(bf16)


def stacked(value):
    return jnp.concatenate(halves(value), axis=0)


def prepare_kernel(rows, pairs, inverse_at, coupling_at, is_first, flip, inv_ref, cpl_ref, bw_ref, dw_ref):
    flipped = flip[0]

    def one_row(row, carry):
        block = inverse_at(inv_ref, jnp.where(flipped == 0, row, rows - 1 - row)).T
        bw_ref[row] = stacked(block)
        return carry

    def one_pair(pair, carry):
        for slot in range(4):
            index = 4 * pair + slot
            block = coupling_at(cpl_ref, jnp.where(flipped == 0, index, 4 * pairs - 1 - index)).T
            row = 2 * pair + 1 - is_first[index]
            high, low = halves(block)
            left = jnp.concatenate([high, high, low], axis=1)
            right = jnp.concatenate([bw_ref[row], bw_ref[row, :BLK]], axis=0)
            product = jnp.dot(left, right, preferred_element_type=f32)
            dw_ref[pair, pl.ds(2 * BLK * slot, 2 * BLK)] = stacked(product)
        return carry

    lax.fori_loop(0, rows, one_row, 0, unroll=4)
    lax.fori_loop(0, pairs, one_pair, 0)


def prepare(rows, pairs, inverse_at, coupling_at, is_first, flip, inv, cpl):
    return pl.pallas_call(
        functools.partial(prepare_kernel, rows, pairs, inverse_at, coupling_at),
        out_shape=(
            pltpu.VMEM((rows, 2 * BLK, BLK), bf16),
            pltpu.VMEM((pairs, 8 * BLK, BLK), bf16),
        ),
        in_specs=[pl.BlockSpec(memory_space=pltpu.SMEM)] * 2 + [pl.BlockSpec(memory_space=pltpu.VMEM)] * 2,
        out_specs=[pl.BlockSpec(memory_space=pltpu.VMEM)] * 2,
        compiler_params=pltpu.CompilerParams(vmem_limit_bytes=24 * 2**20),
        name="prepare",
    )(is_first, flip, inv, cpl)


def wavefront(stages):
    first = min(lo + lag for lag, lo, hi, _ in stages)
    last = max(hi + lag for lag, lo, hi, _ in stages)
    waiting = []
    for turn in range(first, last):
        ready = []
        for lag, lo, hi, item in stages:
            if lo <= turn - lag < hi:
                ready.append(item(turn - lag))
        for store in waiting:
            store()
        waiting = ready
    for store in waiting:
        store()


def inverse_item(weights, u_of, src_ref, rates, h_ref, f_ref, slot, pair):
    results = []
    for row in (2 * pair, 2 * pair + 1):
        u = u_of(row)
        right = u + step_size * (src_ref[pl.ds(row, 1)] - rates * jnp.tanh(u))
        x = stacked(right)
        y = jnp.dot(jnp.concatenate([x, x], axis=1), weights(row), preferred_element_type=f32)
        results.append(y)

    def store():
        for row, y in zip((2 * pair, 2 * pair + 1), results):
            value = y[:S] + y[S:]
            f_ref[slot, row + 1] = value
            h_ref[slot, row + 1] = stacked(value)

    return store


def coupled_item(weights, cols, is_first, h_ref, f_ref, h_slot, f_slot, put, pair):
    zero = jnp.zeros((2 * S, BLK), bf16)
    top, bottom = [], []
    for slot in range(4):
        x = h_ref[h_slot, cols[4 * pair + slot]]
        if slot == 0:
            a, b = x, zero
        elif slot == 3:
            a, b = zero, x
        else:
            mine = is_first[4 * pair + slot].astype(f32).astype(bf16)
            a = x * mine
            b = x - a
        top += [a, a]
        bottom += [b, b]
    left = jnp.concatenate([jnp.concatenate(top, axis=1), jnp.concatenate(bottom, axis=1)], axis=0)
    y = jnp.dot(left, weights(pair), preferred_element_type=f32)

    def store():
        for half, row in enumerate((2 * pair, 2 * pair + 1)):
            part = y[2 * S * half : 2 * S * (half + 1)]
            put(row, f_ref[f_slot, row + 1] - (part[:S] + part[S:]))

    return store


def build_stages(ranges, bw, dw, u_first, put_last, src_ref, rates, cols, is_first, h_ref, f_ref):
    stages = []
    lag = 0
    for step in range(STEPS):
        zeroth, first = 2 * step, 2 * step + 1
        inv_range, mid_range, out_range = ranges(step)
        if step == 0:
            u_of = u_first
        else:
            lag += 2

            def u_of(row, slot=STEPS + step - 1):
                return f_ref[slot, row + 1]

        stages.append(
            (lag, *inv_range, functools.partial(inverse_item, bw, u_of, src_ref, rates, h_ref, f_ref_slot(f_ref), zeroth))
        )
        lag += 3

        def put_mid(row, value, slot=first):
            h_ref[slot, row + 1] = stacked(value)

        stages.append(
            (lag, *mid_range, functools.partial(coupled_item, dw, cols, is_first, h_ref, f_ref, zeroth, step, put_mid))
        )
        lag += 3
        if step == STEPS - 1:
            put = put_last
        else:

            def put(row, value, slot=STEPS + step):
                f_ref[slot, row + 1] = value

        stages.append(
            (lag, *out_range, functools.partial(coupled_item, dw, cols, is_first, h_ref, f_ref, first, step, put))
        )
    return stages


class f_ref_slot:
    def __init__(self, ref):
        self.ref = ref

    def __setitem__(self, index, value):
        self.ref[index[0] // 2, index[1]] = value


def interior_kernel(cols, is_first, rate_ref, src_ref, bw_ref, dw_ref, low_ref, face_ref, h_ref, f_ref, out_ref):
    for slot in range(2 * STEPS):
        h_ref[slot, 0] = jnp.zeros((2 * S, BLK), bf16)

    def u_first(row):
        return low_ref[row] if row < LOW else face_ref[NB - 1 - row]

    def put_last(row, value):
        out_ref[row] = value

    def ranges(step):
        return (0, PAIRS - 2 * step), (0, PAIRS - 2 * step - 1), (0, PAIRS - 2 * step - 2)

    wavefront(
        build_stages(
            ranges, lambda r: bw_ref[r], lambda p: dw_ref[p], u_first, put_last,
            src_ref, rate_ref[...], cols, is_first, h_ref, f_ref,
        )
    )


def border_kernel(
    cols, is_first, rate_ref, src_ref, bw_ref, dw_ref, bg_ref, dg_ref, ghost_ref, h_in, f_in, out_ref, h_ref, f_ref
):
    del h_in, f_in

    def u_first(row):
        return ghost_ref[row - NB]

    def put_last(row, value):
        out_ref[NB - 1 - row] = value

    def ranges(step):
        low, count = PAIRS - 2 * step, 2 * STEPS
        return (low, low + count), (low - 1, low - 1 + count), (low - 2, low - 2 + count)

    def bw(row):
        return bw_ref[row] if row < NB else bg_ref[row - NB]

    def dw(pair):
        return dw_ref[pair] if pair < PAIRS else dg_ref[pair - PAIRS]

    wavefront(
        build_stages(ranges, bw, dw, u_first, put_last, src_ref, rate_ref[...], cols, is_first, h_ref, f_ref)
    )


H_SHAPE = (2 * STEPS, WIN, 2 * S, BLK)
F_SHAPE = (2 * STEPS - 1, WIN, S, BLK)


def pinned(array):
    return pltpu.with_memory_space_constraint(array, pltpu.VMEM)


def interior(cols, is_first, rates, src, bw, dw, low, face):
    vmem, smem = pl.BlockSpec(memory_space=pltpu.VMEM), pl.BlockSpec(memory_space=pltpu.SMEM)
    return pl.pallas_call(
        interior_kernel,
        out_shape=(
            pltpu.VMEM(H_SHAPE, bf16),
            pltpu.VMEM(F_SHAPE, f32),
            pltpu.VMEM((LOW, S, BLK), f32),
        ),
        in_specs=[smem] * 2 + [vmem] * 6,
        out_specs=[vmem] * 3,
        compiler_params=pltpu.CompilerParams(vmem_limit_bytes=8 * 2**20),
        cost_estimate=pl.CostEstimate(flops=4 * 10**9, bytes_accessed=10 * 2**20, transcendentals=0),
        name="interior",
    )(cols, is_first, rates, src, pinned(bw), pinned(dw), pinned(low), face)


def border(cols, is_first, rates, src, bw, dw, bg, dg, ghost, h, f):
    vmem, smem = pl.BlockSpec(memory_space=pltpu.VMEM), pl.BlockSpec(memory_space=pltpu.SMEM)
    out = pl.pallas_call(
        border_kernel,
        out_shape=(
            jax.ShapeDtypeStruct((GROWS, S, BLK), f32),
            pltpu.VMEM(H_SHAPE, bf16),
            pltpu.VMEM(F_SHAPE, f32),
        ),
        in_specs=[smem] * 2 + [vmem] * 9,
        out_specs=[vmem] * 3,
        input_output_aliases={9: 1, 10: 2},
        compiler_params=pltpu.CompilerParams(vmem_limit_bytes=8 * 2**20),
        cost_estimate=pl.CostEstimate(flops=10**9, bytes_accessed=4 * 2**20, transcendentals=0),
        name="border",
    )(cols, is_first, rates, src, pinned(bw), pinned(dw), pinned(bg), pinned(dg), ghost, pinned(h), pinned(f))
    return out[0]


def own_inverse(ref, row):
    return ref[row]


def own_coupling(ref, index):
    return ref[index]


PART_INV, PART_CPL = GROWS // 4, GPAIRS


def ghost_inverse(ref, row):
    return ref[row // PART_INV, row % PART_INV]


def ghost_coupling(ref, index):
    return ref[index // PART_CPL, PART_INV + index % PART_CPL]


def on_device(
    guess_states,
    coarse_rate,
    source,
    reaction_rate,
    inverse_blocks,
    coupling_blocks,
    column_index,
    row_offsets,
):
    tm_count = lax.axis_size("tm")
    mine, slab = lax.axis_index("tm"), lax.axis_index("space")
    core = mine & 1
    both = ("tm", "space")
    swap = [(0, 1), (1, 0)]
    across = [(2 * t + p, 2 * (t ^ 2) + 1 - p) for t in range(tm_count) for p in range(2)]

    def partner(bit):
        return [(t, t ^ (1 << bit)) for t in range(tm_count)]

    def ordered(array):
        return jnp.where(slab == 0, array, array[::-1])

    inv_base = jnp.where(slab == 0, NB - GROWS, 0)
    cpl_base = jnp.where(slab == 0, 4 * (PAIRS - GPAIRS), 0)

    def part(quarter):
        return jnp.concatenate(
            [
                lax.dynamic_slice_in_dim(inverse_blocks, inv_base + PART_INV * quarter, PART_INV, 0),
                lax.dynamic_slice_in_dim(coupling_blocks, cpl_base + PART_CPL * quarter, PART_CPL, 0),
            ],
            axis=0,
        )

    near = lax.ppermute(part(2 * core), "space", swap)
    far = lax.ppermute(part(2 * core + 1), both, across)
    fetched = jnp.stack([near, far])
    other = lax.ppermute(fetched, "tm", partner(0))
    parts = jnp.where(core == 0, jnp.concatenate([fetched, other]), jnp.concatenate([other, fetched]))

    next_rate = lax.ppermute(coarse_rate[0], "tm", [(t, t - 1) for t in range(1, tm_count)])

    positions = jnp.arange(4 * PAIRS, dtype=jnp.int32)
    owner = jnp.sum((row_offsets[0, 1:, None] <= positions[None, :]).astype(jnp.int32), axis=0)
    column = column_index[0]
    own_cols = ordered(jnp.where(slab == 0, column - 1, NB - column))
    own_first = ordered(1 - (jnp.where(slab == 0, owner, NB - 1 - owner) & 1))

    low_face = ordered(guess_states[0].reshape(S, NB, BLK).transpose(1, 0, 2))
    src_own = ordered(source.reshape(NB, BLK))
    sent_cols = (2 * NB - 1 - own_cols[::-1][: 4 * GPAIRS]).astype(f32)
    sent_first = (1 - own_first[::-1][: 4 * GPAIRS]).astype(f32)
    table = jnp.zeros((S, BLK), f32).at[0, : 4 * GPAIRS].set(sent_cols).at[1, : 4 * GPAIRS].set(sent_first)
    face = low_face[LOW:][::-1]
    low = low_face[:LOW]
    src_sent = src_own[LOW:][::-1].reshape(GROWS // S, S, BLK)
    received = lax.ppermute(jnp.concatenate([face, src_sent, table[None]]), "space", swap)
    ghost = received[:GROWS]
    src = jnp.concatenate([src_own, received[GROWS:-1].reshape(GROWS, BLK)])
    cols = jnp.concatenate([own_cols, received[-1, 0, : 4 * GPAIRS].astype(jnp.int32)]) + 1
    is_first = jnp.concatenate([own_first, received[-1, 1, : 4 * GPAIRS].astype(jnp.int32)])
    ghost_first = is_first[4 * PAIRS :]
    flip = jnp.full((1,), slab, jnp.int32)
    rates = jnp.broadcast_to(reaction_rate[:, None], (S, BLK))

    bw, dw = prepare(NB, PAIRS, own_inverse, own_coupling, own_first, flip, inverse_blocks, coupling_blocks)
    bg, dg = prepare(GROWS, GPAIRS, ghost_inverse, ghost_coupling, ghost_first, flip, parts, parts)

    for number in range(ROUNDS):
        if number:
            ghost = lax.ppermute(face, "space", swap)
        h, f, low = interior(cols, is_first, rates, src, bw, dw, low, face)
        face = border(cols, is_first, rates, src, bw, dw, bg, dg, ghost, h, f)
        if number == ROUNDS // 2 - 1:
            relaxed = jnp.concatenate([low, face[::-1]])
    settled = jnp.concatenate([low, face[::-1]])

    decay = ordered((1.0 / (1.0 + next_rate)).reshape(NB, BLK))
    term = settled - decay[:, None, :] * relaxed
    leading = mine == 0
    term = jnp.where(leading, decay[:, None, :] * relaxed + term, term)
    factor = jnp.where(leading, 0.0, decay)

    half = NB // 2

    def packed(factor, term):
        return jnp.concatenate([term, factor.reshape(-1, S, BLK)])

    def unpacked(pack):
        return pack[half:].reshape(half, BLK), pack[:half]

    def of_half(which, array):
        return lax.dynamic_slice_in_dim(array, which * half, half, 0)

    kept = of_half(core, factor), of_half(core, term)
    given = packed(of_half(1 - core, factor), of_half(1 - core, term))
    got = unpacked(lax.ppermute(given, "tm", partner(0)))

    def choose(flag, left, right):
        return jnp.where(flag, left[0], right[0]), jnp.where(flag, left[1], right[1])

    def compose(earlier, later):
        return later[0] * earlier[0], later[0][:, None, :] * earlier[1] + later[1]

    even = choose(core == 0, kept, got)
    odd = choose(core == 0, got, kept)
    total = compose(even, odd)
    prefix = None
    bits = tm_count.bit_length() - 1
    for bit in range(1, bits):
        there = unpacked(lax.ppermute(packed(*total), "tm", partner(bit)))
        upper = ((mine >> bit) & 1) == 1
        neutral = (jnp.ones_like(total[0]), jnp.zeros_like(total[1]))
        added = choose(upper, there, neutral)
        prefix = added if prefix is None else compose(added, prefix)
        if bit < bits - 1:
            total = compose(choose(upper, there, total), choose(upper, total, there))
    first_end = of_half(core, relaxed)
    other_first = lax.ppermute(of_half(1 - core, relaxed), "tm", partner(0))
    chip_leads = (mine >> 1) == 0
    end_even = jnp.where(chip_leads, jnp.where(core == 0, first_end, other_first), prefix[1])
    end_odd = even[0][:, None, :] * prefix[1] + even[1]
    swapped = lax.ppermute(jnp.where(core == 0, end_odd, end_even), "tm", partner(0))
    own = jnp.where(core == 0, end_even, end_odd)
    result = ordered(jnp.where(core == 0, jnp.concatenate([own, swapped]), jnp.concatenate([swapped, own])))
    return result.transpose(1, 0, 2).reshape(1, S, NB * BLK)


def solution(mesh):
    in_specs = (
        P("tm", None, "space"),
        P("tm", "space"),
        P("space"),
        P(),
        P("space", None, None),
        P("space", None, None),
        P("space", None),
        P("space", None),
    )
    out_specs = P("tm", None, "space")
    return jax.shard_map(
        on_device, mesh=mesh, in_specs=in_specs, out_specs=out_specs, check_vma=False
    )
```

```python
import functools

import jax
import jax.numpy as jnp
from jax import lax
from jax.experimental import pallas as pl
from jax.experimental.pallas import tpu as pltpu
from jax.sharding import PartitionSpec as P

M = 8
SWEEPS = 2
STEPS = 2
ROUNDS = 2 * M // STEPS
NB = 32
PAIRS = NB // 2
GROWS = 4 * STEPS
GPAIRS = GROWS // 2 - 1
WIN = NB + GROWS + 1
S = 8
BLK = 128
LOW = NB - GROWS

step_size = 0.25

bf16 = jnp.bfloat16
f32 = jnp.float32


def halves(value):
    high = value.astype(bf16)
    return high, (value - high.astype(f32)).astype(bf16)


def stacked(value):
    return jnp.concatenate(halves(value), axis=0)


def split_row(block, bw_ref, row):
    bw_ref[row] = stacked(block.T)


def multiplied(block, bw_ref, row):
    high, low = halves(block.T)
    left = jnp.concatenate([high, high, low], axis=1)
    right = jnp.concatenate([bw_ref[row], bw_ref[row, :BLK]], axis=0)
    return stacked(jnp.dot(left, right, preferred_element_type=f32))


def own_weights_kernel(is_first, place, inv_hbm, cpl_hbm, bw_ref, dw_ref, inv_ref, cpl_ref, inv_sems, cpl_sems):
    flipped = place[0] == 1
    rows, blocks = NB // CHUNKS, 4 * PAIRS // CHUNKS

    def copies(chunk):
        at = jnp.where(flipped, CHUNKS - 1 - chunk, chunk)
        inv_at, cpl_at = pl.ds(at * rows, rows), pl.ds(at * blocks, blocks)
        return (
            pltpu.make_async_copy(inv_hbm.at[inv_at], inv_ref.at[inv_at], inv_sems.at[chunk]),
            pltpu.make_async_copy(cpl_hbm.at[cpl_at], cpl_ref.at[cpl_at], cpl_sems.at[chunk]),
        )

    for chunk in range(CHUNKS):
        for copy in copies(chunk):
            copy.start()

    def body(chunk, carry):
        for copy in copies(chunk):
            copy.wait()
        for r in range(rows):
            row = rows * chunk + r
            split_row(inv_ref[jnp.where(flipped, NB - 1 - row, row)], bw_ref, row)
        products = []
        for k in range(blocks):
            index = blocks * chunk + k
            row = 2 * (index // 4) + 1 - is_first[index]
            products.append(multiplied(cpl_ref[jnp.where(flipped, 4 * PAIRS - 1 - index, index)], bw_ref, row))
        for k, product in enumerate(products):
            pair = (blocks // 4) * chunk + k // 4
            dw_ref[pair, pl.ds(2 * BLK * (k % 4), 2 * BLK)] = product
        return carry

    lax.fori_loop(0, CHUNKS, body, 0)


CHUNKS = 8


def own_weights(is_first, place, inv, cpl):
    smem, hbm = pl.BlockSpec(memory_space=pltpu.SMEM), pl.BlockSpec(memory_space=pltpu.HBM)
    return pl.pallas_call(
        own_weights_kernel,
        out_shape=(
            pltpu.VMEM((NB, 2 * BLK, BLK), bf16),
            pltpu.VMEM((PAIRS, 8 * BLK, BLK), bf16),
        ),
        in_specs=[smem, smem, hbm, hbm],
        out_specs=[pl.BlockSpec(memory_space=pltpu.VMEM)] * 2,
        scratch_shapes=[
            pltpu.VMEM((NB, BLK, BLK), f32),
            pltpu.VMEM((4 * PAIRS, BLK, BLK), f32),
            pltpu.SemaphoreType.DMA((CHUNKS,)),
            pltpu.SemaphoreType.DMA((CHUNKS,)),
        ],
        compiler_params=pltpu.CompilerParams(vmem_limit_bytes=10 * 2**20),
        name="own_weights",
    )(is_first, place, in_hbm(inv), in_hbm(cpl))


def ghost_weights_kernel(place, received_ref, near, far, other_near, other_far, table, bg_ref, dg_ref, numbers, sem):
    copy = pltpu.make_async_copy(received_ref.at[pl.ds(GROWS + 1, TABLE)], numbers, sem)
    copy.start()
    leads = place[1] == 0

    def block_of(quarter, slot):
        own, other = ((near, other_near), (far, other_far))[quarter % 2]
        if quarter < 2:
            return jnp.where(leads, own[slot], other[slot])
        return jnp.where(leads, other[slot], own[slot])

    for row in range(GROWS):
        split_row(block_of(row // PART_INV, row % PART_INV), bg_ref, row)
    copy.wait()
    for index in range(8 * GPAIRS):
        table[index] = numbers[index // S, index % S, 0].astype(jnp.int32)
    for index in range(4 * GPAIRS):
        row = 2 * (index // 4) + 1 - table[4 * GPAIRS + index]
        product = multiplied(block_of(index // PART_CPL, PART_INV + index % PART_CPL), bg_ref, row)
        dg_ref[index // 4, pl.ds(2 * BLK * (index % 4), 2 * BLK)] = product


PART_INV, PART_CPL = GROWS // 4, GPAIRS
PART = PART_INV + PART_CPL


TABLE = 8 * GPAIRS // S
SENT = GROWS + 1 + TABLE


def ghost_weights(place, received, near, far, other_near, other_far):
    smem, vmem = pl.BlockSpec(memory_space=pltpu.SMEM), pl.BlockSpec(memory_space=pltpu.VMEM)
    return pl.pallas_call(
        ghost_weights_kernel,
        out_shape=(
            jax.ShapeDtypeStruct((8 * GPAIRS,), jnp.int32),
            pltpu.VMEM((GROWS, 2 * BLK, BLK), bf16),
            pltpu.VMEM((GPAIRS, 8 * BLK, BLK), bf16),
        ),
        in_specs=[smem] + [vmem] * 5,
        out_specs=[smem] + [vmem] * 2,
        scratch_shapes=[pltpu.SMEM((TABLE, S, BLK), f32), pltpu.SemaphoreType.DMA],
        compiler_params=pltpu.CompilerParams(vmem_limit_bytes=8 * 2**20),
        name="ghost_weights",
    )(place, received, near, far, other_near, other_far)


def setup_kernel(
    place, offsets, column, rate, guess_hbm, src_ref, inv_hbm, cpl_hbm,
    cols, is_first, rates_ref, low_ref, face_ref, own_src_ref, sent_ref, near_ref, far_ref,
    guess_ref, sem, guess_sem,
):
    flipped = place[0] == 1
    copies = []
    for side, ref in enumerate((near_ref, far_ref)):
        for slot in range(PART):
            if slot < PART_INV:
                row = PART_INV * (2 * place[1] + side) + slot
                source = inv_hbm.at[jnp.where(flipped, row, NB - 1 - row)]
            else:
                index = PART_CPL * (2 * place[1] + side) + slot - PART_INV
                source = cpl_hbm.at[jnp.where(flipped, index, 4 * PAIRS - 1 - index)]
            copies.append(pltpu.make_async_copy(source, ref.at[slot], sem.at[side, slot]))
    guess_copy = pltpu.make_async_copy(guess_hbm, guess_ref, guess_sem)
    guess_copy.start()
    for copy in copies:
        copy.start()
    for index in range(4 * PAIRS):
        stored = jnp.where(flipped, 4 * PAIRS - 1 - index, index)
        pair = index // 4
        first = (stored < offsets[2 * jnp.where(flipped, PAIRS - 1 - pair, pair) + 1]).astype(jnp.int32)
        is_first[index] = jnp.where(flipped, 1 - first, first)
        cols[index] = jnp.where(flipped, NB + 1 - column[stored], column[stored])
    for index in range(4 * GPAIRS):
        mirror = 4 * PAIRS - 1 - index
        for at, value in ((index, 2 * NB + 1 - cols[mirror]), (4 * GPAIRS + index, 1 - is_first[mirror])):
            sent_ref[GROWS + 1 + at // S, pl.ds(at % S, 1)] = jnp.full((1, BLK), value.astype(f32))
    for scenario in range(S):
        rates_ref[pl.ds(scenario, 1)] = jnp.full((1, BLK), rate[scenario])
    for row in range(NB):
        at = jnp.where(flipped, NB - 1 - row, row)
        own_src_ref[pl.ds(row, 1)] = src_ref[pl.ds(at, 1)]
    for row in range(GROWS):
        sent_ref[GROWS, pl.ds(row, 1)] = own_src_ref[pl.ds(NB - 1 - row, 1)]
    guess_copy.wait()
    for row in range(NB):
        block = guess_ref[jnp.where(flipped, NB - 1 - row, row)]
        if row < LOW:
            low_ref[row] = block
        else:
            face_ref[NB - 1 - row] = block
            sent_ref[NB - 1 - row] = block
    for copy in copies:
        copy.wait()


def in_hbm(array):
    return pltpu.with_memory_space_constraint(array, pltpu.HBM)


def setup(place, offsets, column, rate, guess, src, inv, cpl):
    smem, vmem = pl.BlockSpec(memory_space=pltpu.SMEM), pl.BlockSpec(memory_space=pltpu.VMEM)
    hbm = pl.BlockSpec(memory_space=pltpu.HBM)
    return pl.pallas_call(
        setup_kernel,
        out_shape=(
            jax.ShapeDtypeStruct((4 * PAIRS,), jnp.int32),
            jax.ShapeDtypeStruct((4 * PAIRS,), jnp.int32),
            jax.ShapeDtypeStruct((S, BLK), f32),
            jax.ShapeDtypeStruct((LOW, S, BLK), f32),
            jax.ShapeDtypeStruct((GROWS, S, BLK), f32),
            jax.ShapeDtypeStruct((NB, BLK), f32),
            jax.ShapeDtypeStruct((SENT, S, BLK), f32),
            jax.ShapeDtypeStruct((PART, BLK, BLK), f32),
            jax.ShapeDtypeStruct((PART, BLK, BLK), f32),
        ),
        in_specs=[smem] * 4 + [hbm, vmem, hbm, hbm],
        out_specs=[smem] * 2 + [vmem] * 7,
        scratch_shapes=[
            pltpu.VMEM((NB, S, BLK), f32),
            pltpu.SemaphoreType.DMA((2, PART)),
            pltpu.SemaphoreType.DMA,
        ],
        compiler_params=pltpu.CompilerParams(vmem_limit_bytes=4 * 2**20),
        name="setup",
    )(place, offsets, column, rate, in_hbm(guess), src, in_hbm(inv), in_hbm(cpl))


def wavefront(stages):
    first = min(lo + lag for lag, lo, hi, _ in stages)
    last = max(hi + lag for lag, lo, hi, _ in stages)
    waiting = []
    for turn in range(first, last):
        ready = []
        for lag, lo, hi, item in stages:
            if lo <= turn - lag < hi:
                ready.append(item(turn - lag))
        for store in waiting:
            store()
        waiting = ready
    for store in waiting:
        store()


def inverse_item(weights, u_of, src, rates, h_ref, f_ref, slot, pair):
    results = []
    for row in (2 * pair, 2 * pair + 1):
        u = u_of(row)
        right = u + step_size * (src(row) - rates * jnp.tanh(u))
        x = stacked(right)
        y = jnp.dot(jnp.concatenate([x, x], axis=1), weights(row), preferred_element_type=f32)
        results.append(y)

    def store():
        for row, y in zip((2 * pair, 2 * pair + 1), results):
            value = y[:S] + y[S:]
            f_ref[slot, row + 1] = value
            h_ref[slot, row + 1] = stacked(value)

    return store


def coupled_item(weights, cols, is_first, h_ref, f_ref, h_slot, f_slot, put, pair):
    zero = jnp.zeros((2 * S, BLK), bf16)
    top, bottom = [], []
    for slot in range(4):
        x = h_ref[h_slot, cols(4 * pair + slot)]
        if slot == 0:
            a, b = x, zero
        elif slot == 3:
            a, b = zero, x
        else:
            mine = is_first(4 * pair + slot).astype(f32).astype(bf16)
            a = x * mine
            b = x - a
        top += [a, a]
        bottom += [b, b]
    left = jnp.concatenate([jnp.concatenate(top, axis=1), jnp.concatenate(bottom, axis=1)], axis=0)
    y = jnp.dot(left, weights(pair), preferred_element_type=f32)

    def store():
        for half, row in enumerate((2 * pair, 2 * pair + 1)):
            part = y[2 * S * half : 2 * S * (half + 1)]
            put(row, f_ref[f_slot, row + 1] - (part[:S] + part[S:]))

    return store


def build_stages(ranges, bw, dw, u_first, put_last, src, rates, cols, is_first, h_ref, f_ref):
    stages = []
    lag = 0
    for step in range(STEPS):
        zeroth, first = 2 * step, 2 * step + 1
        inv_range, mid_range, out_range = ranges(step)
        if step == 0:
            u_of = u_first
        else:
            lag += 2

            def u_of(row, slot=STEPS + step - 1):
                return f_ref[slot, row + 1]

        stages.append(
            (lag, *inv_range, functools.partial(inverse_item, bw, u_of, src, rates, h_ref, f_ref_slot(f_ref), zeroth))
        )
        lag += 3

        def put_mid(row, value, slot=first):
            h_ref[slot, row + 1] = stacked(value)

        stages.append(
            (lag, *mid_range, functools.partial(coupled_item, dw, cols, is_first, h_ref, f_ref, zeroth, step, put_mid))
        )
        lag += 3
        if step == STEPS - 1:
            put = put_last
        else:

            def put(row, value, slot=STEPS + step):
                f_ref[slot, row + 1] = value

        stages.append(
            (lag, *out_range, functools.partial(coupled_item, dw, cols, is_first, h_ref, f_ref, first, step, put))
        )
    return stages


class f_ref_slot:
    def __init__(self, ref):
        self.ref = ref

    def __setitem__(self, index, value):
        self.ref[index[0] // 2, index[1]] = value


def carried(step):
    base = NB - 4 * step
    return (
        (0, 2 * step, base - 4, base),
        (0, 2 * step + 1, base - 6, base - 2),
        (1, step, base - 4, base),
    )


def interior_kernel(
    cols, is_first, rate_ref, src_ref, bw_ref, dw_ref, low_ref, face_ref, out_ref, kept_h, kept_f, h_ref, f_ref
):
    for slot in range(2 * STEPS):
        h_ref[slot, 0] = jnp.zeros((2 * S, BLK), bf16)

    def u_first(row):
        return low_ref[row] if row < LOW else face_ref[NB - 1 - row]

    def put_last(row, value):
        out_ref[row] = value

    def ranges(step):
        return (0, PAIRS - 2 * step), (0, PAIRS - 2 * step - 1), (0, PAIRS - 2 * step - 2)

    wavefront(
        build_stages(
            ranges, lambda r: bw_ref[r], lambda p: dw_ref[p], u_first, put_last, lambda r: src_ref[pl.ds(r, 1)],
            rate_ref[...], lambda k: cols[k], lambda k: is_first[k], h_ref, f_ref,
        )
    )
    for step in range(STEPS):
        for buffer, slot, first, end in carried(step):
            for row in range(first, end):
                if buffer == 0:
                    kept_h[slot, row - first] = h_ref[slot, row + 1]
                else:
                    kept_f[slot, row - first] = f_ref[slot, row + 1]


def border_kernel(
    cols, is_first, table, rate_ref, src_ref, received_ref, bw_ref, dw_ref, bg_ref, dg_ref, ghost_ref, kept_h, kept_f,
    out_ref, h_ref, f_ref,
):
    for step in range(STEPS):
        for buffer, slot, first, end in carried(step):
            for row in range(first, end):
                if buffer == 0:
                    h_ref[slot, row + 1] = kept_h[slot, row - first]
                else:
                    f_ref[slot, row + 1] = kept_f[slot, row - first]

    def u_first(row):
        return ghost_ref[row - NB]

    def put_last(row, value):
        out_ref[NB - 1 - row] = value

    def ranges(step):
        low, count = PAIRS - 2 * step, 2 * STEPS
        return (low, low + count), (low - 1, low - 1 + count), (low - 2, low - 2 + count)

    def bw(row):
        return bw_ref[row] if row < NB else bg_ref[row - NB]

    def dw(pair):
        return dw_ref[pair] if pair < PAIRS else dg_ref[pair - PAIRS]

    def src(row):
        return src_ref[pl.ds(row, 1)] if row < NB else received_ref[GROWS, pl.ds(row - NB, 1)]

    def col(k):
        return cols[k] if k < 4 * PAIRS else table[k - 4 * PAIRS]

    def first(k):
        return is_first[k] if k < 4 * PAIRS else table[4 * GPAIRS + k - 4 * PAIRS]

    wavefront(build_stages(ranges, bw, dw, u_first, put_last, src, rate_ref[...], col, first, h_ref, f_ref))


SCRATCH = (
    pltpu.VMEM((2 * STEPS, WIN, 2 * S, BLK), bf16),
    pltpu.VMEM((2 * STEPS - 1, WIN, S, BLK), f32),
)


def pinned(array):
    return pltpu.with_memory_space_constraint(array, pltpu.VMEM)


def interior(cols, is_first, rates, src, bw, dw, low, face):
    vmem, smem = pl.BlockSpec(memory_space=pltpu.VMEM), pl.BlockSpec(memory_space=pltpu.SMEM)
    return pl.pallas_call(
        interior_kernel,
        out_shape=(
            jax.ShapeDtypeStruct((LOW, S, BLK), f32),
            jax.ShapeDtypeStruct((2 * STEPS, 4, 2 * S, BLK), bf16),
            jax.ShapeDtypeStruct((STEPS, 4, S, BLK), f32),
        ),
        in_specs=[smem] * 2 + [vmem] * 6,
        out_specs=[vmem] * 3,
        scratch_shapes=SCRATCH,
        compiler_params=pltpu.CompilerParams(vmem_limit_bytes=4 * 2**20),
        cost_estimate=pl.CostEstimate(flops=4 * 10**9, bytes_accessed=10 * 2**20, transcendentals=0),
        name="interior",
    )(cols, is_first, rates, src, pinned(bw), pinned(dw), low, face)


def border(cols, is_first, table, rates, src, received, bw, dw, bg, dg, ghost, kept_h, kept_f):
    vmem, smem = pl.BlockSpec(memory_space=pltpu.VMEM), pl.BlockSpec(memory_space=pltpu.SMEM)
    return pl.pallas_call(
        border_kernel,
        out_shape=jax.ShapeDtypeStruct((GROWS, S, BLK), f32),
        in_specs=[smem] * 3 + [vmem] * 10,
        out_specs=vmem,
        scratch_shapes=SCRATCH,
        compiler_params=pltpu.CompilerParams(vmem_limit_bytes=4 * 2**20),
        cost_estimate=pl.CostEstimate(flops=10**9, bytes_accessed=4 * 2**20, transcendentals=0),
        name="border",
    )(
        cols, is_first, table, rates, src, received, pinned(bw), pinned(dw), pinned(bg), pinned(dg), ghost, kept_h, kept_f
    )


HALF = NB // 2
PACK = HALF + HALF // S


def terms_kernel(place, rate_ref, low_mid, face_mid, low, face, kept_ref, given_ref, relaxed_ref, settled_ref):
    for row in range(NB):
        relaxed_ref[row] = low_mid[row] if row < LOW else face_mid[NB - 1 - row]
        settled_ref[row] = low[row] if row < LOW else face[NB - 1 - row]
    flipped, leads = place[0] == 1, place[2] == 0
    for half, ref in ((place[1], kept_ref), (1 - place[1], given_ref)):
        for i in range(HALF):
            row = HALF * half + i
            decay = 1.0 / (1.0 + rate_ref[pl.ds(jnp.where(flipped, NB - 1 - row, row), 1)])
            carried_on = decay * relaxed_ref[row]
            term = settled_ref[row] - carried_on
            ref[i] = jnp.where(leads, carried_on + term, term)
            ref[HALF + i // S, pl.ds(i % S, 1)] = jnp.where(leads, 0.0, decay)


def terms(place, rate, low_mid, face_mid, low, face):
    vmem = pl.BlockSpec(memory_space=pltpu.VMEM)
    return pl.pallas_call(
        terms_kernel,
        out_shape=(jax.ShapeDtypeStruct((PACK, S, BLK), f32),) * 2,
        in_specs=[pl.BlockSpec(memory_space=pltpu.SMEM)] + [vmem] * 5,
        out_specs=[vmem] * 2,
        scratch_shapes=[pltpu.VMEM((NB, S, BLK), f32)] * 2,
        compiler_params=pltpu.CompilerParams(vmem_limit_bytes=2 * 2**20),
        name="terms",
    )(place, rate, low_mid, face_mid, low, face)


def assemble_kernel(place, own, swapped, low_mid, face_mid, out_ref):
    flipped, leads, core = place[0] == 1, place[2] == 0, place[1]
    for row in range(NB):
        half, i = row // HALF, row % HALF
        value = jnp.where(core == half, own[i], swapped[i])
        first = low_mid[row] if row < LOW else face_mid[NB - 1 - row]
        out_ref[jnp.where(flipped, NB - 1 - row, row)] = jnp.where(leads, first, value)


def assemble(place, own, swapped, low_mid, face_mid):
    vmem = pl.BlockSpec(memory_space=pltpu.VMEM)
    return pl.pallas_call(
        assemble_kernel,
        out_shape=jax.ShapeDtypeStruct((NB, S, BLK), f32),
        in_specs=[pl.BlockSpec(memory_space=pltpu.SMEM)] + [vmem] * 4,
        out_specs=vmem,
        compiler_params=pltpu.CompilerParams(vmem_limit_bytes=2 * 2**20),
        name="assemble",
    )(place, own, swapped, low_mid, face_mid)


def on_device(
    guess_states,
    coarse_rate,
    source,
    reaction_rate,
    inverse_blocks,
    coupling_blocks,
    column_index,
    row_offsets,
):
    tm_count = lax.axis_size("tm")
    mine, slab = lax.axis_index("tm"), lax.axis_index("space")
    core = mine & 1
    both = ("tm", "space")
    swap = [(0, 1), (1, 0)]
    across = [(2 * t + p, 2 * (t ^ 2) + 1 - p) for t in range(tm_count) for p in range(2)]

    def partner(bit):
        return [(t, t ^ (1 << bit)) for t in range(tm_count)]

    place = jnp.stack([slab, core, mine]).astype(jnp.int32)
    cols, is_first, rates, low, face, src, sent, near_sent, far_sent = setup(
        place, row_offsets[0], column_index[0], reaction_rate,
        guess_states[0].reshape(S, NB, BLK).transpose(1, 0, 2), source.reshape(NB, BLK),
        inverse_blocks, coupling_blocks,
    )
    received = lax.ppermute(sent, "space", swap)
    near = lax.ppermute(near_sent, "space", swap)
    far = lax.ppermute(far_sent, both, across)

    bw, dw = own_weights(is_first, place, inverse_blocks, coupling_blocks)
    other_near, other_far = (lax.ppermute(quarter, "tm", partner(0)) for quarter in (near, far))
    table, bg, dg = ghost_weights(place, received, near, far, other_near, other_far)

    held = []
    ghost = received
    next_rate = coarse_rate
    for number in range(ROUNDS):
        if number:
            ghost = lax.ppermute(face, "space", swap)
        if number == 1:
            face, next_rate = lax.optimization_barrier((face, next_rate))
            next_rate = lax.ppermute(next_rate[0], "tm", [(t, t - 1) for t in range(1, tm_count)])
        low, kept_h, kept_f = interior(cols, is_first, rates, src, bw, dw, low, face)
        face = border(cols, is_first, table, rates, src, received, bw, dw, bg, dg, ghost, kept_h, kept_f)
        if number % (ROUNDS // 2) == ROUNDS // 2 - 1:
            held += [low, face]

    def unpacked(pack):
        return pack[HALF:].reshape(HALF, BLK), pack[:HALF]

    def packed(factor, term):
        return jnp.concatenate([term, factor.reshape(-1, S, BLK)])

    def choose(flag, left, right):
        return jnp.where(flag, left[0], right[0]), jnp.where(flag, left[1], right[1])

    def compose(earlier, later):
        return later[0] * earlier[0], later[0][:, None, :] * earlier[1] + later[1]

    kept, given = terms(place, next_rate.reshape(NB, BLK), *held)
    kept, got = unpacked(kept), unpacked(lax.ppermute(given, "tm", partner(0)))
    even = choose(core == 0, kept, got)
    odd = choose(core == 0, got, kept)
    total = compose(even, odd)
    prefix = None
    bits = tm_count.bit_length() - 1
    for bit in range(1, bits):
        there = unpacked(lax.ppermute(packed(*total), "tm", partner(bit)))
        upper = ((mine >> bit) & 1) == 1
        neutral = (jnp.ones_like(total[0]), jnp.zeros_like(total[1]))
        added = choose(upper, there, neutral)
        prefix = added if prefix is None else compose(added, prefix)
        if bit < bits - 1:
            total = compose(choose(upper, there, total), choose(upper, total, there))
    end_odd = even[0][:, None, :] * prefix[1] + even[1]
    swapped = lax.ppermute(jnp.where(core == 0, end_odd, prefix[1]), "tm", partner(0))
    result = assemble(place, jnp.where(core == 0, prefix[1], end_odd), swapped, *held[:2])
    return result.transpose(1, 0, 2).reshape(1, S, NB * BLK)


def solution(mesh):
    in_specs = (
        P("tm", None, "space"),
        P("tm", "space"),
        P("space"),
        P(),
        P("space", None, None),
        P("space", None, None),
        P("space", None),
        P("space", None),
    )
    out_specs = P("tm", None, "space")
    return jax.shard_map(
        on_device, mesh=mesh, in_specs=in_specs, out_specs=out_specs, check_vma=False
    )
```

```python
import functools

import jax
import jax.numpy as jnp
from jax import lax
from jax.experimental import pallas as pl
from jax.experimental.pallas import tpu as pltpu
from jax.sharding import PartitionSpec as P

M = 8
SWEEPS = 2
STEPS = 4
ROUNDS = 2 * M // STEPS
NB = 32
PAIRS = NB // 2
GROWS = 4 * STEPS
GPAIRS = GROWS // 2 - 1
WIN = NB + GROWS + 1
S = 8
BLK = 128
LOW = NB - GROWS

step_size = 0.25

bf16 = jnp.bfloat16
f32 = jnp.float32


def halves(value):
    high = value.astype(bf16)
    return high, (value - high.astype(f32)).astype(bf16)


def stacked(value):
    return jnp.concatenate(halves(value), axis=0)


def split_row(block, bw_ref, row):
    bw_ref[row] = stacked(block.T)


def multiplied(block, bw_ref, row):
    high, low = halves(block.T)
    left = jnp.concatenate([high, high, low], axis=1)
    right = jnp.concatenate([bw_ref[row], bw_ref[row, :BLK]], axis=0)
    return stacked(jnp.dot(left, right, preferred_element_type=f32))


def own_weights_kernel(
    place, offsets_hbm, column_hbm, rate_hbm, guess_hbm, src_hbm, inv_hbm, cpl_hbm,
    cols, is_first, rates_ref, low_ref, face_ref, own_src_ref, sent_ref, bw_ref, dw_ref,
    offsets, column, rate, guess_ref, src_ref, inv_ref, cpl_ref, inv_sems, cpl_sems, sems,
):
    flipped = place[0] == 1
    rows, blocks = NB // CHUNKS, 4 * PAIRS // CHUNKS
    small = [
        pltpu.make_async_copy(source, target, sems.at[number])
        for number, (source, target) in enumerate(
            (
                (offsets_hbm, offsets), (column_hbm, column), (rate_hbm, rate), (src_hbm, src_ref), (guess_hbm, guess_ref),
            )
        )
    ]

    def copies(chunk):
        at = jnp.where(flipped, CHUNKS - 1 - chunk, chunk)
        inv_at, cpl_at = pl.ds(at * rows, rows), pl.ds(at * blocks, blocks)
        return (
            pltpu.make_async_copy(inv_hbm.at[inv_at], inv_ref.at[inv_at], inv_sems.at[chunk]),
            pltpu.make_async_copy(cpl_hbm.at[cpl_at], cpl_ref.at[cpl_at], cpl_sems.at[chunk]),
        )

    for copy in small:
        copy.start()
    for chunk in range(CHUNKS):
        for copy in copies(chunk):
            copy.start()
    for copy in small:
        copy.wait()
    for index in range(4 * PAIRS):
        stored = jnp.where(flipped, 4 * PAIRS - 1 - index, index)
        pair = jnp.where(flipped, PAIRS - 1 - index // 4, index // 4)
        first = (stored < offsets[0, 2 * pair + 1]).astype(jnp.int32)
        is_first[index] = jnp.where(flipped, 1 - first, first)
        cols[index] = jnp.where(flipped, NB + 1 - column[0, stored], column[0, stored])
    for index in range(4 * GPAIRS):
        mirror = 4 * PAIRS - 1 - index
        for at, value in ((index, 2 * NB + 1 - cols[mirror]), (4 * GPAIRS + index, 1 - is_first[mirror])):
            sent_ref[GROWS + SRC_TILES + at // S, pl.ds(at % S, 1)] = jnp.full((1, BLK), value.astype(f32))
    for scenario in range(S):
        rates_ref[pl.ds(scenario, 1)] = jnp.full((1, BLK), rate[scenario])
    for row in range(NB):
        at = jnp.where(flipped, NB - 1 - row, row)
        own_src_ref[pl.ds(row, 1)] = src_ref[pl.ds(at, 1)]
    for row in range(GROWS):
        sent_ref[GROWS + row // S, pl.ds(row % S, 1)] = own_src_ref[pl.ds(NB - 1 - row, 1)]
    for row in range(NB):
        block = guess_ref[jnp.where(flipped, NB - 1 - row, row)]
        if row < LOW:
            low_ref[row] = block
        else:
            face_ref[NB - 1 - row] = block
            sent_ref[NB - 1 - row] = block

    def body(chunk, carry):
        for copy in copies(chunk):
            copy.wait()
        for r in range(rows):
            row = rows * chunk + r
            split_row(inv_ref[jnp.where(flipped, NB - 1 - row, row)], bw_ref, row)
        products = []
        for k in range(blocks):
            index = blocks * chunk + k
            row = 2 * (index // 4) + 1 - is_first[index]
            products.append(multiplied(cpl_ref[jnp.where(flipped, 4 * PAIRS - 1 - index, index)], bw_ref, row))
        for k, product in enumerate(products):
            pair = (blocks // 4) * chunk + k // 4
            dw_ref[pair, pl.ds(2 * BLK * (k % 4), 2 * BLK)] = product
        return carry

    lax.fori_loop(0, CHUNKS, body, 0)


CHUNKS = 8


def own_weights(place, offsets, column, rate, guess, src, inv, cpl):
    smem, vmem = pl.BlockSpec(memory_space=pltpu.SMEM), pl.BlockSpec(memory_space=pltpu.VMEM)
    given = (offsets, column, rate, guess, src, inv, cpl)
    return pl.pallas_call(
        own_weights_kernel,
        out_shape=(
            jax.ShapeDtypeStruct((4 * PAIRS,), jnp.int32),
            jax.ShapeDtypeStruct((4 * PAIRS,), jnp.int32),
            jax.ShapeDtypeStruct((S, BLK), f32),
            jax.ShapeDtypeStruct((LOW, S, BLK), f32),
            jax.ShapeDtypeStruct((GROWS, S, BLK), f32),
            jax.ShapeDtypeStruct((NB, BLK), f32),
            jax.ShapeDtypeStruct((SENT, S, BLK), f32),
            pltpu.VMEM((NB, 2 * BLK, BLK), bf16),
            pltpu.VMEM((PAIRS, 8 * BLK, BLK), bf16),
        ),
        in_specs=[smem] + [pl.BlockSpec(memory_space=pltpu.HBM)] * 7,
        out_specs=[smem] * 2 + [vmem] * 7,
        scratch_shapes=[
            pltpu.SMEM(offsets.shape, jnp.int32),
            pltpu.SMEM(column.shape, jnp.int32),
            pltpu.SMEM(rate.shape, f32),
            pltpu.VMEM(guess.shape, f32),
            pltpu.VMEM(src.shape, f32),
            pltpu.VMEM(inv.shape, f32),
            pltpu.VMEM(cpl.shape, f32),
            pltpu.SemaphoreType.DMA((CHUNKS,)),
            pltpu.SemaphoreType.DMA((CHUNKS,)),
            pltpu.SemaphoreType.DMA((5,)),
        ],
        compiler_params=pltpu.CompilerParams(vmem_limit_bytes=10 * 2**20),
        cost_estimate=pl.CostEstimate(flops=10**10, bytes_accessed=12 * 2**20, transcendentals=0),
        name="own_weights",
    )(place, *(in_hbm(array) for array in given))


def ghost_weights_kernel(place, received_ref, near, far, other_near, other_far, table, bg_ref, dg_ref, numbers, sem):
    copy = pltpu.make_async_copy(received_ref.at[pl.ds(GROWS + SRC_TILES, TABLE)], numbers, sem)
    copy.start()
    leads = place[1] == 0

    def block_of(quarter, slot):
        own, other = ((near, other_near), (far, other_far))[quarter % 2]
        if quarter < 2:
            return jnp.where(leads, own[slot], other[slot])
        return jnp.where(leads, other[slot], own[slot])

    for row in range(GROWS):
        split_row(block_of(row // PART_INV, row % PART_INV), bg_ref, row)
    copy.wait()
    for index in range(8 * GPAIRS):
        table[index] = numbers[index // S, index % S, 0].astype(jnp.int32)
    for index in range(4 * GPAIRS):
        row = 2 * (index // 4) + 1 - table[4 * GPAIRS + index]
        product = multiplied(block_of(index // PART_CPL, PART_INV + index % PART_CPL), bg_ref, row)
        dg_ref[index // 4, pl.ds(2 * BLK * (index % 4), 2 * BLK)] = product


PART_INV, PART_CPL = GROWS // 4, GPAIRS
PART = PART_INV + PART_CPL


SRC_TILES = GROWS // S
TABLE = 8 * GPAIRS // S
SENT = GROWS + SRC_TILES + TABLE


def ghost_weights(place, received, near, far, other_near, other_far):
    smem, vmem = pl.BlockSpec(memory_space=pltpu.SMEM), pl.BlockSpec(memory_space=pltpu.VMEM)
    return pl.pallas_call(
        ghost_weights_kernel,
        out_shape=(
            jax.ShapeDtypeStruct((8 * GPAIRS,), jnp.int32),
            pltpu.VMEM((GROWS, 2 * BLK, BLK), bf16),
            pltpu.VMEM((GPAIRS, 8 * BLK, BLK), bf16),
        ),
        in_specs=[smem] + [vmem] * 5,
        out_specs=[smem] + [vmem] * 2,
        scratch_shapes=[pltpu.SMEM((TABLE, S, BLK), f32), pltpu.SemaphoreType.DMA],
        compiler_params=pltpu.CompilerParams(vmem_limit_bytes=8 * 2**20),
        cost_estimate=pl.CostEstimate(flops=3 * 10**9, bytes_accessed=5 * 2**20, transcendentals=0),
        name="ghost_weights",
    )(place, received, near, far, other_near, other_far)


def face_weights_kernel(place, inv_hbm, cpl_hbm, near_ref, far_ref, sem):
    flipped = place[0] == 1
    copies = []
    for side, ref in enumerate((near_ref, far_ref)):
        for slot in range(PART):
            if slot < PART_INV:
                row = PART_INV * (2 * place[1] + side) + slot
                source = inv_hbm.at[jnp.where(flipped, row, NB - 1 - row)]
            else:
                index = PART_CPL * (2 * place[1] + side) + slot - PART_INV
                source = cpl_hbm.at[jnp.where(flipped, index, 4 * PAIRS - 1 - index)]
            copies.append(pltpu.make_async_copy(source, ref.at[slot], sem.at[side, slot]))
    for copy in copies:
        copy.start()
    for copy in copies:
        copy.wait()


def in_hbm(array):
    return pltpu.with_memory_space_constraint(array, pltpu.HBM)


def face_weights(place, inv, cpl):
    hbm, vmem = pl.BlockSpec(memory_space=pltpu.HBM), pl.BlockSpec(memory_space=pltpu.VMEM)
    return pl.pallas_call(
        face_weights_kernel,
        out_shape=(jax.ShapeDtypeStruct((PART, BLK, BLK), f32),) * 2,
        in_specs=[pl.BlockSpec(memory_space=pltpu.SMEM), hbm, hbm],
        out_specs=[vmem] * 2,
        scratch_shapes=[pltpu.SemaphoreType.DMA((2, PART))],
        compiler_params=pltpu.CompilerParams(vmem_limit_bytes=2 * 2**20),
        name="face_weights",
    )(place, in_hbm(inv), in_hbm(cpl))


def wavefront(stages, late):
    first = min(lo + lag for lag, lo, hi, _ in stages)
    last = max(hi + lag for lag, lo, hi, _ in stages)
    waiting = []
    for turn in range(first, last):
        ready = []
        for lag, lo, hi, item in stages:
            if lo <= turn - lag < hi:
                ready.append(item(turn - lag))
        if late:
            waiting, ready = ready, waiting
        for store in ready:
            store()
    for store in waiting:
        store()


def inverse_item(weights, u_of, src, rates, h_ref, f_ref, slot, pair):
    results = []
    for row in (2 * pair, 2 * pair + 1):
        u = u_of(row)
        right = u + step_size * (src(row) - rates * jnp.tanh(u))
        x = stacked(right)
        y = jnp.dot(jnp.concatenate([x, x], axis=1), weights(row), preferred_element_type=f32)
        results.append(y)

    def store():
        for row, y in zip((2 * pair, 2 * pair + 1), results):
            value = y[:S] + y[S:]
            f_ref[slot, row + 1] = value
            h_ref[slot, row + 1] = stacked(value)

    return store


def coupled_item(weights, cols, is_first, h_ref, f_ref, h_slot, f_slot, put, pair):
    zero = jnp.zeros((2 * S, BLK), bf16)
    top, bottom = [], []
    for slot in range(4):
        x = h_ref[h_slot, cols(4 * pair + slot)]
        if slot == 0:
            a, b = x, zero
        elif slot == 3:
            a, b = zero, x
        else:
            mine = is_first(4 * pair + slot).astype(f32).astype(bf16)
            a = x * mine
            b = x - a
        top += [a, a]
        bottom += [b, b]
    left = jnp.concatenate([jnp.concatenate(top, axis=1), jnp.concatenate(bottom, axis=1)], axis=0)
    y = jnp.dot(left, weights(pair), preferred_element_type=f32)

    def store():
        for half, row in enumerate((2 * pair, 2 * pair + 1)):
            part = y[2 * S * half : 2 * S * (half + 1)]
            put(row, f_ref[f_slot, row + 1] - (part[:S] + part[S:]))

    return store


def build_stages(ranges, bw, dw, u_first, put_last, src, rates, cols, is_first, h_ref, f_ref, late):
    stages = []
    lag = 0
    for step in range(STEPS):
        zeroth, first = 2 * step, 2 * step + 1
        inv_range, mid_range, out_range = ranges(step)
        if step == 0:
            u_of = u_first
        else:
            lag += 1 + late

            def u_of(row, slot=STEPS + step - 1):
                return f_ref[slot, row + 1]

        stages.append(
            (lag, *inv_range, functools.partial(inverse_item, bw, u_of, src, rates, h_ref, f_ref_slot(f_ref), zeroth))
        )
        lag += 2 + late

        def put_mid(row, value, slot=first):
            h_ref[slot, row + 1] = stacked(value)

        stages.append(
            (lag, *mid_range, functools.partial(coupled_item, dw, cols, is_first, h_ref, f_ref, zeroth, step, put_mid))
        )
        lag += 2 + late
        if step == STEPS - 1:
            put = put_last
        else:

            def put(row, value, slot=STEPS + step):
                f_ref[slot, row + 1] = value

        stages.append(
            (lag, *out_range, functools.partial(coupled_item, dw, cols, is_first, h_ref, f_ref, first, step, put))
        )
    return stages


class f_ref_slot:
    def __init__(self, ref):
        self.ref = ref

    def __setitem__(self, index, value):
        self.ref[index[0] // 2, index[1]] = value


def carried(step):
    base = NB - 4 * step
    return (
        (0, 2 * step, base - 4, base),
        (0, 2 * step + 1, base - 6, base - 2),
        (1, step, base - 4, base),
    )


def interior_kernel(
    cols, is_first, rate_ref, src_ref, bw_ref, dw_ref, low_ref, face_ref, out_ref, kept_h, kept_f, h_ref, f_ref
):
    for slot in range(2 * STEPS):
        h_ref[slot, 0] = jnp.zeros((2 * S, BLK), bf16)

    def u_first(row):
        return low_ref[row] if row < LOW else face_ref[NB - 1 - row]

    def put_last(row, value):
        out_ref[row] = value

    def ranges(step):
        return (0, PAIRS - 2 * step), (0, PAIRS - 2 * step - 1), (0, PAIRS - 2 * step - 2)

    wavefront(
        build_stages(
            ranges, lambda r: bw_ref[r], lambda p: dw_ref[p], u_first, put_last, lambda r: src_ref[pl.ds(r, 1)],
            rate_ref[...], lambda k: cols[k], lambda k: is_first[k], h_ref, f_ref, 1,
        ),
        1,
    )
    for step in range(STEPS):
        for buffer, slot, first, end in carried(step):
            for row in range(first, end):
                if buffer == 0:
                    kept_h[slot, row - first] = h_ref[slot, row + 1]
                else:
                    kept_f[slot, row - first] = f_ref[slot, row + 1]


def border_kernel(
    cols, is_first, table, rate_ref, src_ref, received_ref, bw_ref, dw_ref, bg_ref, dg_ref, ghost_ref, kept_h, kept_f,
    out_ref, h_ref, f_ref,
):
    for step in range(STEPS):
        for buffer, slot, first, end in carried(step):
            for row in range(first, end):
                if buffer == 0:
                    h_ref[slot, row + 1] = kept_h[slot, row - first]
                else:
                    f_ref[slot, row + 1] = kept_f[slot, row - first]

    def u_first(row):
        return ghost_ref[row - NB]

    def put_last(row, value):
        out_ref[NB - 1 - row] = value

    def ranges(step):
        low, count = PAIRS - 2 * step, 2 * STEPS
        return (low, low + count), (low - 1, low - 1 + count), (low - 2, low - 2 + count)

    def bw(row):
        return bw_ref[row] if row < NB else bg_ref[row - NB]

    def dw(pair):
        return dw_ref[pair] if pair < PAIRS else dg_ref[pair - PAIRS]

    def src(row):
        return src_ref[pl.ds(row, 1)] if row < NB else received_ref[GROWS + (row - NB) // S, pl.ds((row - NB) % S, 1)]

    def col(k):
        return cols[k] if k < 4 * PAIRS else table[k - 4 * PAIRS]

    def first(k):
        return is_first[k] if k < 4 * PAIRS else table[4 * GPAIRS + k - 4 * PAIRS]

    wavefront(build_stages(ranges, bw, dw, u_first, put_last, src, rate_ref[...], col, first, h_ref, f_ref, 1), 1)


SCRATCH = (
    pltpu.VMEM((2 * STEPS, WIN, 2 * S, BLK), bf16),
    pltpu.VMEM((2 * STEPS - 1, WIN, S, BLK), f32),
)


def pinned(array):
    return pltpu.with_memory_space_constraint(array, pltpu.VMEM)


def interior(cols, is_first, rates, src, bw, dw, low, face):
    vmem, smem = pl.BlockSpec(memory_space=pltpu.VMEM), pl.BlockSpec(memory_space=pltpu.SMEM)
    return pl.pallas_call(
        interior_kernel,
        out_shape=(
            jax.ShapeDtypeStruct((LOW, S, BLK), f32),
            jax.ShapeDtypeStruct((2 * STEPS, 4, 2 * S, BLK), bf16),
            jax.ShapeDtypeStruct((STEPS, 4, S, BLK), f32),
        ),
        in_specs=[smem] * 2 + [vmem] * 6,
        out_specs=[vmem] * 3,
        scratch_shapes=SCRATCH,
        compiler_params=pltpu.CompilerParams(vmem_limit_bytes=4 * 2**20),
        cost_estimate=pl.CostEstimate(flops=6 * 10**9, bytes_accessed=10 * 2**20, transcendentals=0),
        name="interior",
    )(cols, is_first, rates, src, pinned(bw), pinned(dw), low, face)


def border(cols, is_first, table, rates, src, received, bw, dw, bg, dg, ghost, kept_h, kept_f):
    vmem, smem = pl.BlockSpec(memory_space=pltpu.VMEM), pl.BlockSpec(memory_space=pltpu.SMEM)
    return pl.pallas_call(
        border_kernel,
        out_shape=jax.ShapeDtypeStruct((GROWS, S, BLK), f32),
        in_specs=[smem] * 3 + [vmem] * 10,
        out_specs=vmem,
        scratch_shapes=SCRATCH,
        compiler_params=pltpu.CompilerParams(vmem_limit_bytes=4 * 2**20),
        cost_estimate=pl.CostEstimate(flops=4 * 10**9, bytes_accessed=8 * 2**20, transcendentals=0),
        name="border",
    )(
        cols, is_first, table, rates, src, received, pinned(bw), pinned(dw), pinned(bg), pinned(dg), ghost, kept_h, kept_f
    )


HALF = NB // 2
PACK = HALF + HALF // S


def terms_kernel(place, rate_ref, low_mid, face_mid, low, face, kept_ref, given_ref, relaxed_ref, settled_ref):
    for row in range(NB):
        relaxed_ref[row] = low_mid[row] if row < LOW else face_mid[NB - 1 - row]
        settled_ref[row] = low[row] if row < LOW else face[NB - 1 - row]
    flipped, leads = place[0] == 1, place[2] == 0
    for half, ref in ((place[1], kept_ref), (1 - place[1], given_ref)):
        for i in range(HALF):
            row = HALF * half + i
            decay = 1.0 / (1.0 + rate_ref[pl.ds(jnp.where(flipped, NB - 1 - row, row), 1)])
            carried_on = decay * relaxed_ref[row]
            term = settled_ref[row] - carried_on
            ref[i] = jnp.where(leads, carried_on + term, term)
            ref[HALF + i // S, pl.ds(i % S, 1)] = jnp.where(leads, 0.0, decay)


def terms(place, rate, low_mid, face_mid, low, face):
    vmem = pl.BlockSpec(memory_space=pltpu.VMEM)
    return pl.pallas_call(
        terms_kernel,
        out_shape=(jax.ShapeDtypeStruct((PACK, S, BLK), f32),) * 2,
        in_specs=[pl.BlockSpec(memory_space=pltpu.SMEM)] + [vmem] * 5,
        out_specs=[vmem] * 2,
        scratch_shapes=[pltpu.VMEM((NB, S, BLK), f32)] * 2,
        compiler_params=pltpu.CompilerParams(vmem_limit_bytes=2 * 2**20),
        name="terms",
    )(place, rate, low_mid, face_mid, low, face)


def assemble_kernel(place, own, swapped, low_mid, face_mid, out_ref):
    flipped, leads, core = place[0] == 1, place[2] == 0, place[1]
    for row in range(NB):
        half, i = row // HALF, row % HALF
        value = jnp.where(core == half, own[i], swapped[i])
        first = low_mid[row] if row < LOW else face_mid[NB - 1 - row]
        out_ref[jnp.where(flipped, NB - 1 - row, row)] = jnp.where(leads, first, value)


def assemble(place, own, swapped, low_mid, face_mid):
    vmem = pl.BlockSpec(memory_space=pltpu.VMEM)
    return pl.pallas_call(
        assemble_kernel,
        out_shape=jax.ShapeDtypeStruct((NB, S, BLK), f32),
        in_specs=[pl.BlockSpec(memory_space=pltpu.SMEM)] + [vmem] * 4,
        out_specs=vmem,
        compiler_params=pltpu.CompilerParams(vmem_limit_bytes=2 * 2**20),
        name="assemble",
    )(place, own, swapped, low_mid, face_mid)


def on_device(
    guess_states,
    coarse_rate,
    source,
    reaction_rate,
    inverse_blocks,
    coupling_blocks,
    column_index,
    row_offsets,
):
    tm_count = lax.axis_size("tm")
    mine, slab = lax.axis_index("tm"), lax.axis_index("space")
    core = mine & 1
    both = ("tm", "space")
    swap = [(0, 1), (1, 0)]
    across = [(2 * t + p, 2 * (t ^ 2) + 1 - p) for t in range(tm_count) for p in range(2)]

    def partner(bit):
        return [(t, t ^ (1 << bit)) for t in range(tm_count)]

    place = jnp.stack([slab, core, mine]).astype(jnp.int32)
    near_sent, far_sent = face_weights(place, inverse_blocks, coupling_blocks)
    near = lax.ppermute(near_sent, "space", swap)
    far = lax.ppermute(far_sent, both, across)
    cols, is_first, rates, low, face, src, sent, bw, dw = own_weights(
        place, row_offsets, column_index, reaction_rate,
        guess_states[0].reshape(S, NB, BLK).transpose(1, 0, 2), source.reshape(NB, BLK),
        inverse_blocks, coupling_blocks,
    )
    received = lax.ppermute(sent, "space", swap)
    held = []
    for number in range(ROUNDS):
        ghost = lax.ppermute(face, "space", swap) if number else received
        low, kept_h, kept_f = interior(cols, is_first, rates, src, bw, dw, low, face)
        if not number:
            near, far, next_rate, kept_f = lax.optimization_barrier((near, far, coarse_rate, kept_f))
            other_near, other_far = (lax.ppermute(quarter, "tm", partner(0)) for quarter in (near, far))
            next_rate = lax.ppermute(next_rate[0], "tm", [(t, t - 1) for t in range(1, tm_count)])
            table, bg, dg = ghost_weights(place, received, near, far, other_near, other_far)
        face = border(cols, is_first, table, rates, src, received, bw, dw, bg, dg, ghost, kept_h, kept_f)
        if number % (ROUNDS // 2) == ROUNDS // 2 - 1:
            held += [low, face]

    def unpacked(pack):
        return pack[HALF:].reshape(HALF, BLK), pack[:HALF]

    def packed(factor, term):
        return jnp.concatenate([term, factor.reshape(-1, S, BLK)])

    def choose(flag, left, right):
        return jnp.where(flag, left[0], right[0]), jnp.where(flag, left[1], right[1])

    def compose(earlier, later):
        return later[0] * earlier[0], later[0][:, None, :] * earlier[1] + later[1]

    kept, given = terms(place, next_rate.reshape(NB, BLK), *held)
    kept, got = unpacked(kept), unpacked(lax.ppermute(given, "tm", partner(0)))
    even = choose(core == 0, kept, got)
    odd = choose(core == 0, got, kept)
    total = compose(even, odd)
    neutral = (jnp.ones_like(total[0]), jnp.zeros_like(total[1]))
    prefix = neutral
    bits = tm_count.bit_length() - 1
    for bit in range(1, bits, 2):
        pack = packed(*total)
        one, two, three = (
            unpacked(lax.ppermute(pack, "tm", [(t, t ^ (mask << bit)) for t in range(tm_count)]))
            for mask in (1, 2, 3)
        )
        odd_place, upper = ((mine >> bit) & 1) == 1, ((mine >> (bit + 1)) & 1) == 1
        near_total = compose(choose(odd_place, one, total), choose(odd_place, total, one))
        far_total = compose(choose(odd_place, three, two), choose(odd_place, two, three))
        added = compose(choose(upper, far_total, neutral), choose(odd_place, one, neutral))
        prefix = compose(added, prefix)
        total = compose(choose(upper, far_total, near_total), choose(upper, near_total, far_total))
    end_odd = even[0][:, None, :] * prefix[1] + even[1]
    swapped = lax.ppermute(jnp.where(core == 0, end_odd, prefix[1]), "tm", partner(0))
    result = assemble(place, jnp.where(core == 0, prefix[1], end_odd), swapped, *held[:2])
    return result.transpose(1, 0, 2).reshape(1, S, NB * BLK)


def solution(mesh):
    in_specs = (
        P("tm", None, "space"),
        P("tm", "space"),
        P("space"),
        P(),
        P("space", None, None),
        P("space", None, None),
        P("space", None),
        P("space", None),
    )
    out_specs = P("tm", None, "space")
    return jax.shard_map(
        on_device, mesh=mesh, in_specs=in_specs, out_specs=out_specs, check_vma=False
    )
```

```python
import functools

import jax
import jax.numpy as jnp
from jax import lax
from jax.experimental import pallas as pl
from jax.experimental.pallas import tpu as pltpu
from jax.sharding import PartitionSpec as P

M = 8
SWEEPS = 2
STEPS = 4
ROUNDS = 2 * M // STEPS
NB = 32
PAIRS = NB // 2
GROWS = 4 * STEPS
GPAIRS = GROWS // 2 - 1
WIN = NB + GROWS + 1
S = 8
BLK = 128
LOW = NB - GROWS

step_size = 0.25

bf16 = jnp.bfloat16
f32 = jnp.float32


def halves(value):
    high = value.astype(bf16)
    return high, (value - high.astype(f32)).astype(bf16)


def stacked(value):
    return jnp.concatenate(halves(value), axis=0)


def split_row(block, bw_ref, row):
    bw_ref[row] = stacked(block.T)


def multiplied(block, bw_ref, row):
    high, low = halves(block.T)
    left = jnp.concatenate([high, high, low], axis=1)
    right = jnp.concatenate([bw_ref[row], bw_ref[row, :BLK]], axis=0)
    return stacked(jnp.dot(left, right, preferred_element_type=f32))


def own_weights_kernel(
    place, offsets_hbm, column_hbm, rate_hbm, guess_hbm, src_hbm, inv_hbm, cpl_hbm,
    cols, is_first, rates_ref, low_ref, face_ref, own_src_ref, sent_ref, bw_ref, dw_ref,
    offsets, column, rate, guess_ref, src_ref, inv_ref, cpl_ref, inv_sems, cpl_sems, sems,
):
    flipped = place[0] == 1
    rows, blocks = NB // CHUNKS, 4 * PAIRS // CHUNKS
    small = [
        pltpu.make_async_copy(source, target, sems.at[number])
        for number, (source, target) in enumerate(
            (
                (offsets_hbm, offsets), (column_hbm, column), (rate_hbm, rate), (src_hbm, src_ref), (guess_hbm, guess_ref),
            )
        )
    ]

    def copies(chunk):
        at = jnp.where(flipped, CHUNKS - 1 - chunk, chunk)
        inv_at, cpl_at = pl.ds(at * rows, rows), pl.ds(at * blocks, blocks)
        return (
            pltpu.make_async_copy(inv_hbm.at[inv_at], inv_ref.at[inv_at], inv_sems.at[chunk]),
            pltpu.make_async_copy(cpl_hbm.at[cpl_at], cpl_ref.at[cpl_at], cpl_sems.at[chunk]),
        )

    for copy in small:
        copy.start()
    for chunk in range(CHUNKS):
        for copy in copies(chunk):
            copy.start()
    for copy in small:
        copy.wait()
    for index in range(4 * PAIRS):
        stored = jnp.where(flipped, 4 * PAIRS - 1 - index, index)
        pair = jnp.where(flipped, PAIRS - 1 - index // 4, index // 4)
        first = (stored < offsets[0, 2 * pair + 1]).astype(jnp.int32)
        is_first[index] = jnp.where(flipped, 1 - first, first)
        cols[index] = jnp.where(flipped, NB + 1 - column[0, stored], column[0, stored])
    lane = lax.broadcasted_iota(jnp.int32, (S, BLK), 1)
    line = jnp.zeros((S, BLK), f32)
    for index in range(4 * GPAIRS):
        mirror = 4 * PAIRS - 1 - index
        for at, value in ((index, 2 * NB + 1 - cols[mirror]), (4 * GPAIRS + index, 1 - is_first[mirror])):
            line = jnp.where(lane == at, value.astype(f32), line)
    sent_ref[GROWS + SRC_TILES] = line
    for scenario in range(S):
        rates_ref[pl.ds(scenario, 1)] = jnp.full((1, BLK), rate[scenario])
    for row in range(NB):
        at = jnp.where(flipped, NB - 1 - row, row)
        own_src_ref[pl.ds(row, 1)] = src_ref[pl.ds(at, 1)]
    for row in range(GROWS):
        sent_ref[GROWS + row // S, pl.ds(row % S, 1)] = own_src_ref[pl.ds(NB - 1 - row, 1)]
    for row in range(NB):
        block = guess_ref[jnp.where(flipped, NB - 1 - row, row)]
        if row < LOW:
            low_ref[row] = block
        else:
            face_ref[NB - 1 - row] = block
            sent_ref[NB - 1 - row] = block

    def body(chunk, carry):
        for copy in copies(chunk):
            copy.wait()
        for r in range(rows):
            row = rows * chunk + r
            split_row(inv_ref[jnp.where(flipped, NB - 1 - row, row)], bw_ref, row)
        products = []
        for k in range(blocks):
            index = blocks * chunk + k
            row = 2 * (index // 4) + 1 - is_first[index]
            products.append(multiplied(cpl_ref[jnp.where(flipped, 4 * PAIRS - 1 - index, index)], bw_ref, row))
        for k, product in enumerate(products):
            pair = (blocks // 4) * chunk + k // 4
            dw_ref[pair, pl.ds(2 * BLK * (k % 4), 2 * BLK)] = product
        return carry

    lax.fori_loop(0, CHUNKS, body, 0)


CHUNKS = 8


def own_weights(place, offsets, column, rate, guess, src, inv, cpl):
    smem, vmem = pl.BlockSpec(memory_space=pltpu.SMEM), pl.BlockSpec(memory_space=pltpu.VMEM)
    given = (offsets, column, rate, guess, src, inv, cpl)
    return pl.pallas_call(
        own_weights_kernel,
        out_shape=(
            jax.ShapeDtypeStruct((4 * PAIRS,), jnp.int32),
            jax.ShapeDtypeStruct((4 * PAIRS,), jnp.int32),
            jax.ShapeDtypeStruct((S, BLK), f32),
            jax.ShapeDtypeStruct((LOW, S, BLK), f32),
            jax.ShapeDtypeStruct((GROWS, S, BLK), f32),
            jax.ShapeDtypeStruct((NB, BLK), f32),
            jax.ShapeDtypeStruct((SENT, S, BLK), f32),
            pltpu.VMEM((NB, 2 * BLK, BLK), bf16),
            pltpu.VMEM((PAIRS, 8 * BLK, BLK), bf16),
        ),
        in_specs=[smem] + [pl.BlockSpec(memory_space=pltpu.HBM)] * 7,
        out_specs=[smem] * 2 + [vmem] * 7,
        scratch_shapes=[
            pltpu.SMEM(offsets.shape, jnp.int32),
            pltpu.SMEM(column.shape, jnp.int32),
            pltpu.SMEM(rate.shape, f32),
            pltpu.VMEM(guess.shape, f32),
            pltpu.VMEM(src.shape, f32),
            pltpu.VMEM(inv.shape, f32),
            pltpu.VMEM(cpl.shape, f32),
            pltpu.SemaphoreType.DMA((CHUNKS,)),
            pltpu.SemaphoreType.DMA((CHUNKS,)),
            pltpu.SemaphoreType.DMA((5,)),
        ],
        compiler_params=pltpu.CompilerParams(vmem_limit_bytes=10 * 2**20),
        cost_estimate=pl.CostEstimate(flops=10**10, bytes_accessed=12 * 2**20, transcendentals=0),
        name="own_weights",
    )(place, *(in_hbm(array) for array in given))


def ghost_weights_kernel(batch, place, numbers_in, near, far, other_near, other_far, *refs):
    rows, pairs = BATCHES[batch]
    leads = place[1] == 0
    if batch:
        table, (bg_ref, dg_ref) = numbers_in, refs
    else:
        table, bg_ref, dg_ref, numbers, sem = refs
        copy = pltpu.make_async_copy(numbers_in.at[GROWS + SRC_TILES], numbers, sem)
        copy.start()

    def block_of(quarter, slot):
        own, other = ((near, other_near), (far, other_far))[quarter % 2]
        if quarter < 2:
            return jnp.where(leads, own[slot], other[slot])
        return jnp.where(leads, other[slot], own[slot])

    for row in range(rows):
        split_row(block_of(row // (rows // 4), row % (rows // 4)), bg_ref, row)
    if not batch:
        copy.wait()
        for index in range(8 * GPAIRS):
            table[index] = numbers[0, index].astype(jnp.int32)
    base = 4 * GPAIRS + 4 * sum(count for _, count in BATCHES[:batch])
    for index in range(4 * pairs):
        row = 2 * (index // 4) + 1 - table[base + index]
        product = multiplied(block_of(index // pairs, rows // 4 + index % pairs), bg_ref, row)
        dg_ref[index // 4, pl.ds(2 * BLK * (index % 4), 2 * BLK)] = product


SRC_TILES = GROWS // S
SENT = GROWS + SRC_TILES + 1


def ghost_weights(batch, place, numbers, *parts):
    smem, vmem = pl.BlockSpec(memory_space=pltpu.SMEM), pl.BlockSpec(memory_space=pltpu.VMEM)
    rows, pairs = BATCHES[batch]
    first = not batch
    return pl.pallas_call(
        functools.partial(ghost_weights_kernel, batch),
        out_shape=[jax.ShapeDtypeStruct((8 * GPAIRS,), jnp.int32)] * first
        + [pltpu.VMEM((rows, 2 * BLK, BLK), bf16), pltpu.VMEM((pairs, 8 * BLK, BLK), bf16)],
        in_specs=[smem, vmem if first else smem] + [vmem] * 4,
        out_specs=[smem] * first + [vmem] * 2,
        scratch_shapes=[pltpu.SMEM((S, BLK), f32), pltpu.SemaphoreType.DMA] * first,
        compiler_params=pltpu.CompilerParams(vmem_limit_bytes=8 * 2**20),
        cost_estimate=pl.CostEstimate(flops=2 * 10**9, bytes_accessed=3 * 2**20, transcendentals=0),
        name="ghost_weights",
    )(place, numbers, *parts)


BATCHES = ((2 * ((GPAIRS + 1) // 2), (GPAIRS + 1) // 2), (GROWS - 2 * ((GPAIRS + 1) // 2), GPAIRS // 2))


def face_weights_kernel(place, inv_hbm, cpl_hbm, *refs):
    *parts, sem = refs
    flipped = place[0] == 1
    copies = []
    row_base = index_base = 0
    for batch, (rows, pairs) in enumerate(BATCHES):
        for side in range(2):
            quarter = 2 * place[1] + side
            ref = parts[2 * batch + side]
            for slot in range(rows // 4 + pairs):
                if slot < rows // 4:
                    row = row_base + rows // 4 * quarter + slot
                    source = inv_hbm.at[jnp.where(flipped, row, NB - 1 - row)]
                else:
                    index = index_base + pairs * quarter + slot - rows // 4
                    source = cpl_hbm.at[jnp.where(flipped, index, 4 * PAIRS - 1 - index)]
                copies.append(pltpu.make_async_copy(source, ref.at[slot], sem.at[len(copies)]))
        row_base, index_base = row_base + rows, index_base + 4 * pairs
    for copy in copies:
        copy.start()
    for copy in copies:
        copy.wait()


def in_hbm(array):
    return pltpu.with_memory_space_constraint(array, pltpu.HBM)


def face_weights(place, inv, cpl):
    hbm, vmem = pl.BlockSpec(memory_space=pltpu.HBM), pl.BlockSpec(memory_space=pltpu.VMEM)
    sizes = [rows // 4 + pairs for rows, pairs in BATCHES for _ in range(2)]
    return pl.pallas_call(
        face_weights_kernel,
        out_shape=tuple(jax.ShapeDtypeStruct((size, BLK, BLK), f32) for size in sizes),
        in_specs=[pl.BlockSpec(memory_space=pltpu.SMEM), hbm, hbm],
        out_specs=[vmem] * 4,
        scratch_shapes=[pltpu.SemaphoreType.DMA((sum(sizes),))],
        compiler_params=pltpu.CompilerParams(vmem_limit_bytes=4 * 2**20),
        name="face_weights",
    )(place, in_hbm(inv), in_hbm(cpl))


def wavefront(stages, late):
    first = min(lo + lag for lag, lo, hi, _ in stages)
    last = max(hi + lag for lag, lo, hi, _ in stages)
    waiting = []
    for turn in range(first, last):
        ready = []
        for lag, lo, hi, item in stages:
            if lo <= turn - lag < hi:
                ready.append(item(turn - lag))
        if late:
            waiting, ready = ready, waiting
        for store in ready:
            store()
    for store in waiting:
        store()


def inverse_item(weights, u_of, src, rates, h_ref, f_ref, slot, pair):
    results = []
    for row in (2 * pair, 2 * pair + 1):
        u = u_of(row)
        right = u + step_size * (src(row) - rates * jnp.tanh(u))
        x = stacked(right)
        y = jnp.dot(jnp.concatenate([x, x], axis=1), weights(row), preferred_element_type=f32)
        results.append(y)

    def store():
        for row, y in zip((2 * pair, 2 * pair + 1), results):
            value = y[:S] + y[S:]
            f_ref[slot, row + 1] = value
            h_ref[slot, row + 1] = stacked(value)

    return store


def coupled_item(weights, cols, is_first, h_ref, f_ref, h_slot, f_slot, put, pair):
    zero = jnp.zeros((2 * S, BLK), bf16)
    top, bottom = [], []
    for slot in range(4):
        x = h_ref[h_slot, cols(4 * pair + slot)]
        if slot == 0:
            a, b = x, zero
        elif slot == 3:
            a, b = zero, x
        else:
            mine = is_first(4 * pair + slot).astype(f32).astype(bf16)
            a = x * mine
            b = x - a
        top += [a, a]
        bottom += [b, b]
    left = jnp.concatenate([jnp.concatenate(top, axis=1), jnp.concatenate(bottom, axis=1)], axis=0)
    y = jnp.dot(left, weights(pair), preferred_element_type=f32)

    def store():
        for half, row in enumerate((2 * pair, 2 * pair + 1)):
            part = y[2 * S * half : 2 * S * (half + 1)]
            put(row, f_ref[f_slot, row + 1] - (part[:S] + part[S:]))

    return store


def build_stages(ranges, bw, dw, u_first, put_last, src, rates, cols, is_first, h_ref, f_ref, late):
    stages = []
    lag = 0
    for step in range(STEPS):
        zeroth, first = 2 * step, 2 * step + 1
        inv_range, mid_range, out_range = ranges(step)
        if step == 0:
            u_of = u_first
        else:
            lag += 1 + late

            def u_of(row, slot=STEPS + step - 1):
                return f_ref[slot, row + 1]

        stages.append(
            (lag, *inv_range, functools.partial(inverse_item, bw, u_of, src, rates, h_ref, f_ref_slot(f_ref), zeroth))
        )
        lag += 2 + late

        def put_mid(row, value, slot=first):
            h_ref[slot, row + 1] = stacked(value)

        stages.append(
            (lag, *mid_range, functools.partial(coupled_item, dw, cols, is_first, h_ref, f_ref, zeroth, step, put_mid))
        )
        lag += 2 + late
        if step == STEPS - 1:
            put = put_last
        else:

            def put(row, value, slot=STEPS + step):
                f_ref[slot, row + 1] = value

        stages.append(
            (lag, *out_range, functools.partial(coupled_item, dw, cols, is_first, h_ref, f_ref, first, step, put))
        )
    return stages


class f_ref_slot:
    def __init__(self, ref):
        self.ref = ref

    def __setitem__(self, index, value):
        self.ref[index[0] // 2, index[1]] = value


def carried(step):
    base = NB - 4 * step
    return (
        (0, 2 * step, base - 4, base),
        (0, 2 * step + 1, base - 6, base - 2),
        (1, step, base - 4, base),
    )


def interior_kernel(
    cols, is_first, rate_ref, src_ref, bw_ref, dw_ref, low_ref, face_ref, out_ref, kept_h, kept_f, h_ref, f_ref
):
    for slot in range(2 * STEPS):
        h_ref[slot, 0] = jnp.zeros((2 * S, BLK), bf16)

    def u_first(row):
        return low_ref[row] if row < LOW else face_ref[NB - 1 - row]

    def put_last(row, value):
        out_ref[row] = value

    def ranges(step):
        return (0, PAIRS - 2 * step), (0, PAIRS - 2 * step - 1), (0, PAIRS - 2 * step - 2)

    wavefront(
        build_stages(
            ranges, lambda r: bw_ref[r], lambda p: dw_ref[p], u_first, put_last, lambda r: src_ref[pl.ds(r, 1)],
            rate_ref[...], lambda k: cols[k], lambda k: is_first[k], h_ref, f_ref, 1,
        ),
        1,
    )
    for step in range(STEPS):
        for buffer, slot, first, end in carried(step):
            for row in range(first, end):
                if buffer == 0:
                    kept_h[slot, row - first] = h_ref[slot, row + 1]
                else:
                    kept_f[slot, row - first] = f_ref[slot, row + 1]


def border_kernel(
    cols, is_first, table, rate_ref, src_ref, received_ref, bw_ref, dw_ref, bg0_ref, dg0_ref, bg1_ref, dg1_ref, ghost_ref,
    kept_h, kept_f,
    out_ref, h_ref, f_ref,
):
    for step in range(STEPS):
        for buffer, slot, first, end in carried(step):
            for row in range(first, end):
                if buffer == 0:
                    h_ref[slot, row + 1] = kept_h[slot, row - first]
                else:
                    f_ref[slot, row + 1] = kept_f[slot, row - first]

    def u_first(row):
        return ghost_ref[row - NB]

    def put_last(row, value):
        out_ref[NB - 1 - row] = value

    def ranges(step):
        low, count = PAIRS - 2 * step, 2 * STEPS
        return (low, low + count), (low - 1, low - 1 + count), (low - 2, low - 2 + count)

    def bw(row):
        if row < NB:
            return bw_ref[row]
        return bg0_ref[row - NB] if row - NB < BATCHES[0][0] else bg1_ref[row - NB - BATCHES[0][0]]

    def dw(pair):
        if pair < PAIRS:
            return dw_ref[pair]
        return dg0_ref[pair - PAIRS] if pair - PAIRS < BATCHES[0][1] else dg1_ref[pair - PAIRS - BATCHES[0][1]]

    def src(row):
        return src_ref[pl.ds(row, 1)] if row < NB else received_ref[GROWS + (row - NB) // S, pl.ds((row - NB) % S, 1)]

    def col(k):
        return cols[k] if k < 4 * PAIRS else table[k - 4 * PAIRS]

    def first(k):
        return is_first[k] if k < 4 * PAIRS else table[4 * GPAIRS + k - 4 * PAIRS]

    wavefront(build_stages(ranges, bw, dw, u_first, put_last, src, rate_ref[...], col, first, h_ref, f_ref, 1), 1)


SCRATCH = (
    pltpu.VMEM((2 * STEPS, WIN, 2 * S, BLK), bf16),
    pltpu.VMEM((2 * STEPS - 1, WIN, S, BLK), f32),
)


def pinned(array):
    return pltpu.with_memory_space_constraint(array, pltpu.VMEM)


def interior(cols, is_first, rates, src, bw, dw, low, face):
    vmem, smem = pl.BlockSpec(memory_space=pltpu.VMEM), pl.BlockSpec(memory_space=pltpu.SMEM)
    return pl.pallas_call(
        interior_kernel,
        out_shape=(
            jax.ShapeDtypeStruct((LOW, S, BLK), f32),
            jax.ShapeDtypeStruct((2 * STEPS, 4, 2 * S, BLK), bf16),
            jax.ShapeDtypeStruct((STEPS, 4, S, BLK), f32),
        ),
        in_specs=[smem] * 2 + [vmem] * 6,
        out_specs=[vmem] * 3,
        scratch_shapes=SCRATCH,
        compiler_params=pltpu.CompilerParams(vmem_limit_bytes=4 * 2**20),
        cost_estimate=pl.CostEstimate(flops=6 * 10**9, bytes_accessed=10 * 2**20, transcendentals=0),
        name="interior",
    )(cols, is_first, rates, src, pinned(bw), pinned(dw), low, face)


def border(cols, is_first, table, rates, src, received, weights, ghost, kept_h, kept_f):
    vmem, smem = pl.BlockSpec(memory_space=pltpu.VMEM), pl.BlockSpec(memory_space=pltpu.SMEM)
    return pl.pallas_call(
        border_kernel,
        out_shape=jax.ShapeDtypeStruct((GROWS, S, BLK), f32),
        in_specs=[smem] * 3 + [vmem] * 12,
        out_specs=vmem,
        scratch_shapes=SCRATCH,
        compiler_params=pltpu.CompilerParams(vmem_limit_bytes=4 * 2**20),
        cost_estimate=pl.CostEstimate(flops=4 * 10**9, bytes_accessed=8 * 2**20, transcendentals=0),
        name="border",
    )(
        cols, is_first, table, rates, src, received, *(pinned(array) for array in weights), ghost, kept_h, kept_f
    )


HALF = NB // 2
PACK = HALF + HALF // S


def terms_kernel(place, rate_ref, low_mid, face_mid, low, face, kept_ref, given_ref, relaxed_ref, settled_ref):
    for row in range(NB):
        relaxed_ref[row] = low_mid[row] if row < LOW else face_mid[NB - 1 - row]
        settled_ref[row] = low[row] if row < LOW else face[NB - 1 - row]
    flipped, leads = place[0] == 1, place[2] == 0
    for half, ref in ((place[1], kept_ref), (1 - place[1], given_ref)):
        for i in range(HALF):
            row = HALF * half + i
            decay = 1.0 / (1.0 + rate_ref[pl.ds(jnp.where(flipped, NB - 1 - row, row), 1)])
            carried_on = decay * relaxed_ref[row]
            term = settled_ref[row] - carried_on
            ref[i] = jnp.where(leads, carried_on + term, term)
            ref[HALF + i // S, pl.ds(i % S, 1)] = jnp.where(leads, 0.0, decay)


def terms(place, rate, low_mid, face_mid, low, face):
    vmem = pl.BlockSpec(memory_space=pltpu.VMEM)
    return pl.pallas_call(
        terms_kernel,
        out_shape=(jax.ShapeDtypeStruct((PACK, S, BLK), f32),) * 2,
        in_specs=[pl.BlockSpec(memory_space=pltpu.SMEM)] + [vmem] * 5,
        out_specs=[vmem] * 2,
        scratch_shapes=[pltpu.VMEM((NB, S, BLK), f32)] * 2,
        compiler_params=pltpu.CompilerParams(vmem_limit_bytes=2 * 2**20),
        name="terms",
    )(place, rate, low_mid, face_mid, low, face)


def assemble_kernel(place, own, swapped, low_mid, face_mid, out_ref):
    flipped, leads, core = place[0] == 1, place[2] == 0, place[1]
    for row in range(NB):
        half, i = row // HALF, row % HALF
        value = jnp.where(core == half, own[i], swapped[i])
        first = low_mid[row] if row < LOW else face_mid[NB - 1 - row]
        out_ref[jnp.where(flipped, NB - 1 - row, row)] = jnp.where(leads, first, value)


def assemble(place, own, swapped, low_mid, face_mid):
    vmem = pl.BlockSpec(memory_space=pltpu.VMEM)
    return pl.pallas_call(
        assemble_kernel,
        out_shape=jax.ShapeDtypeStruct((NB, S, BLK), f32),
        in_specs=[pl.BlockSpec(memory_space=pltpu.SMEM)] + [vmem] * 4,
        out_specs=vmem,
        compiler_params=pltpu.CompilerParams(vmem_limit_bytes=2 * 2**20),
        name="assemble",
    )(place, own, swapped, low_mid, face_mid)


def on_device(
    guess_states,
    coarse_rate,
    source,
    reaction_rate,
    inverse_blocks,
    coupling_blocks,
    column_index,
    row_offsets,
):
    tm_count = lax.axis_size("tm")
    mine, slab = lax.axis_index("tm"), lax.axis_index("space")
    core = mine & 1
    both = ("tm", "space")
    swap = [(0, 1), (1, 0)]
    across = [(2 * t + p, 2 * (t ^ 2) + 1 - p) for t in range(tm_count) for p in range(2)]

    def partner(bit):
        return [(t, t ^ (1 << bit)) for t in range(tm_count)]

    place = jnp.stack([slab, core, mine]).astype(jnp.int32)
    parts = [
        lax.ppermute(part, *(("space", swap), (both, across))[number % 2])
        for number, part in enumerate(face_weights(place, inverse_blocks, coupling_blocks))
    ]
    cols, is_first, rates, low, face, src, sent, bw, dw = own_weights(
        place, row_offsets, column_index, reaction_rate,
        guess_states[0].reshape(S, NB, BLK).transpose(1, 0, 2), source.reshape(NB, BLK),
        inverse_blocks, coupling_blocks,
    )
    received = lax.ppermute(sent, "space", swap)
    def shared(arrays):
        return [*arrays, *(lax.ppermute(array, "tm", partner(0)) for array in arrays)]

    near, far, low = lax.optimization_barrier((*parts[:2], low))
    batch = shared((near, far))
    held = []
    for number in range(ROUNDS):
        ghost = lax.ppermute(face, "space", swap) if number else received
        low, kept_h, kept_f = interior(cols, is_first, rates, src, bw, dw, low, face)
        if not number:
            batch[0], kept_f = lax.optimization_barrier((batch[0], kept_f))
            table, bg0, dg0 = ghost_weights(0, place, received, *batch)
            near, far, next_rate, bg0 = lax.optimization_barrier((*parts[2:], coarse_rate, bg0))
            batch = shared((near, far))
            next_rate = lax.ppermute(next_rate[0], "tm", [(t, t - 1) for t in range(1, tm_count)])
            bg1, dg1 = ghost_weights(1, place, table, *batch)
            weights = (bw, dw, bg0, dg0, bg1, dg1)
        face = border(cols, is_first, table, rates, src, received, weights, ghost, kept_h, kept_f)
        if number % (ROUNDS // 2) == ROUNDS // 2 - 1:
            held += [low, face]

    def unpacked(pack):
        return pack[HALF:].reshape(HALF, BLK), pack[:HALF]

    def packed(factor, term):
        return jnp.concatenate([term, factor.reshape(-1, S, BLK)])

    def choose(flag, left, right):
        return jnp.where(flag, left[0], right[0]), jnp.where(flag, left[1], right[1])

    def compose(earlier, later):
        return later[0] * earlier[0], later[0][:, None, :] * earlier[1] + later[1]

    kept, given = terms(place, next_rate.reshape(NB, BLK), *held)
    kept, got = unpacked(kept), unpacked(lax.ppermute(given, "tm", partner(0)))
    even = choose(core == 0, kept, got)
    odd = choose(core == 0, got, kept)
    total = compose(even, odd)
    neutral = (jnp.ones_like(total[0]), jnp.zeros_like(total[1]))
    prefix = neutral
    bits = tm_count.bit_length() - 1
    for bit in range(1, bits, 2):
        pack = packed(*total)
        three, two, one = (
            unpacked(lax.ppermute(pack, "tm", [(t, t ^ (mask << bit)) for t in range(tm_count)]))
            for mask in (3, 2, 1)
        )
        odd_place, upper = ((mine >> bit) & 1) == 1, ((mine >> (bit + 1)) & 1) == 1
        near_total = compose(choose(odd_place, one, total), choose(odd_place, total, one))
        far_total = compose(choose(odd_place, three, two), choose(odd_place, two, three))
        added = compose(choose(upper, far_total, neutral), choose(odd_place, one, neutral))
        prefix = compose(added, prefix)
        total = compose(choose(upper, far_total, near_total), choose(upper, near_total, far_total))
    end_odd = even[0][:, None, :] * prefix[1] + even[1]
    swapped = lax.ppermute(jnp.where(core == 0, end_odd, prefix[1]), "tm", partner(0))
    result = assemble(place, jnp.where(core == 0, prefix[1], end_odd), swapped, *held[:2])
    return result.transpose(1, 0, 2).reshape(1, S, NB * BLK)


def solution(mesh):
    in_specs = (
        P("tm", None, "space"),
        P("tm", "space"),
        P("space"),
        P(),
        P("space", None, None),
        P("space", None, None),
        P("space", None),
        P("space", None),
    )
    out_specs = P("tm", None, "space")
    return jax.shard_map(
        on_device, mesh=mesh, in_specs=in_specs, out_specs=out_specs, check_vma=False
    )
```

```python
import functools

import jax
import jax.numpy as jnp
from jax import lax
from jax.experimental import pallas as pl
from jax.experimental.pallas import tpu as pltpu
from jax.sharding import PartitionSpec as P

M = 8
SWEEPS = 2
STEPS = 4
ROUNDS = 2 * M // STEPS
NB = 32
PAIRS = NB // 2
GROWS = 4 * STEPS
GPAIRS = GROWS // 2 - 1
WIN = NB + GROWS + 1
S = 8
BLK = 128
LOW = NB - GROWS

step_size = 0.25

bf16 = jnp.bfloat16
f32 = jnp.float32


def halves(value):
    high = value.astype(bf16)
    return high, (value - high.astype(f32)).astype(bf16)


def stacked(value):
    return jnp.concatenate(halves(value), axis=0)


def split_row(block, bw_ref, row):
    bw_ref[row] = stacked(block.T)


def multiplied(block, bw_ref, row):
    high, low = halves(block.T)
    left = jnp.concatenate([high, high, low], axis=1)
    right = jnp.concatenate([bw_ref[row], bw_ref[row, :BLK]], axis=0)
    return stacked(jnp.dot(left, right, preferred_element_type=f32))


def own_weights_kernel(
    place, offsets_hbm, column_hbm, rate_hbm, guess_hbm, src_hbm, inv_hbm, cpl_hbm,
    cols, is_first, rates_ref, low_ref, face_ref, own_src_ref, sent_ref, near_ref, far_ref, bw_ref, dw_ref,
    offsets, column, rate, guess_ref, src_ref, inv_ref, cpl_ref, inv_sems, cpl_sems, sems, face_sems,
):
    flipped = place[0] == 1
    rows, blocks = NB // CHUNKS, 4 * PAIRS // CHUNKS
    small = [
        pltpu.make_async_copy(source, target, sems.at[number])
        for number, (source, target) in enumerate(
            (
                (offsets_hbm, offsets), (column_hbm, column), (rate_hbm, rate), (src_hbm, src_ref), (guess_hbm, guess_ref),
            )
        )
    ]

    def copies(chunk):
        at = jnp.where(flipped, CHUNKS - 1 - chunk, chunk)
        inv_at, cpl_at = pl.ds(at * rows, rows), pl.ds(at * blocks, blocks)
        return (
            pltpu.make_async_copy(inv_hbm.at[inv_at], inv_ref.at[inv_at], inv_sems.at[chunk]),
            pltpu.make_async_copy(cpl_hbm.at[cpl_at], cpl_ref.at[cpl_at], cpl_sems.at[chunk]),
        )

    for copy in small:
        copy.start()
    for chunk in range(CHUNKS):
        for copy in copies(chunk):
            copy.start()
    face_parts = face_copies(1, place, inv_hbm, cpl_hbm, (near_ref, far_ref), face_sems)
    for copy in face_parts:
        copy.start()
    for copy in small:
        copy.wait()
    for index in range(4 * PAIRS):
        stored = jnp.where(flipped, 4 * PAIRS - 1 - index, index)
        pair = jnp.where(flipped, PAIRS - 1 - index // 4, index // 4)
        first = (stored < offsets[0, 2 * pair + 1]).astype(jnp.int32)
        is_first[index] = jnp.where(flipped, 1 - first, first)
        cols[index] = jnp.where(flipped, NB + 1 - column[0, stored], column[0, stored])
    lane = lax.broadcasted_iota(jnp.int32, (S, BLK), 1)
    line = jnp.zeros((S, BLK), f32)
    for index in range(4 * GPAIRS):
        mirror = 4 * PAIRS - 1 - index
        for at, value in ((index, 2 * NB + 1 - cols[mirror]), (4 * GPAIRS + index, 1 - is_first[mirror])):
            line = jnp.where(lane == at, value.astype(f32), line)
    sent_ref[GROWS + SRC_TILES] = line
    for scenario in range(S):
        rates_ref[pl.ds(scenario, 1)] = jnp.full((1, BLK), rate[scenario])
    for row in range(NB):
        at = jnp.where(flipped, NB - 1 - row, row)
        own_src_ref[pl.ds(row, 1)] = src_ref[pl.ds(at, 1)]
    for row in range(GROWS):
        sent_ref[GROWS + row // S, pl.ds(row % S, 1)] = own_src_ref[pl.ds(NB - 1 - row, 1)]
    for row in range(NB):
        block = guess_ref[jnp.where(flipped, NB - 1 - row, row)]
        if row < LOW:
            low_ref[row] = block
        else:
            face_ref[NB - 1 - row] = block
            sent_ref[NB - 1 - row] = block

    def body(chunk, carry):
        for copy in copies(chunk):
            copy.wait()
        for r in range(rows):
            row = rows * chunk + r
            split_row(inv_ref[jnp.where(flipped, NB - 1 - row, row)], bw_ref, row)
        products = []
        for k in range(blocks):
            index = blocks * chunk + k
            row = 2 * (index // 4) + 1 - is_first[index]
            products.append(multiplied(cpl_ref[jnp.where(flipped, 4 * PAIRS - 1 - index, index)], bw_ref, row))
        for k, product in enumerate(products):
            pair = (blocks // 4) * chunk + k // 4
            dw_ref[pair, pl.ds(2 * BLK * (k % 4), 2 * BLK)] = product
        return carry

    lax.fori_loop(0, CHUNKS, body, 0)
    for copy in face_parts:
        copy.wait()


CHUNKS = 4


def own_weights(place, offsets, column, rate, guess, src, inv, cpl):
    smem, vmem = pl.BlockSpec(memory_space=pltpu.SMEM), pl.BlockSpec(memory_space=pltpu.VMEM)
    given = (offsets, column, rate, guess, src, inv, cpl)
    return pl.pallas_call(
        own_weights_kernel,
        out_shape=(
            jax.ShapeDtypeStruct((4 * PAIRS,), jnp.int32),
            jax.ShapeDtypeStruct((4 * PAIRS,), jnp.int32),
            jax.ShapeDtypeStruct((S, BLK), f32),
            jax.ShapeDtypeStruct((LOW, S, BLK), f32),
            jax.ShapeDtypeStruct((GROWS, S, BLK), f32),
            jax.ShapeDtypeStruct((NB, BLK), f32),
            jax.ShapeDtypeStruct((SENT, S, BLK), f32),
            jax.ShapeDtypeStruct((SIZES[1], BLK, BLK), f32),
            jax.ShapeDtypeStruct((SIZES[1], BLK, BLK), f32),
            pltpu.VMEM((NB, 2 * BLK, BLK), bf16),
            pltpu.VMEM((PAIRS, 8 * BLK, BLK), bf16),
        ),
        in_specs=[smem] + [pl.BlockSpec(memory_space=pltpu.HBM)] * 7,
        out_specs=[smem] * 2 + [vmem] * 9,
        scratch_shapes=[
            pltpu.SMEM(offsets.shape, jnp.int32),
            pltpu.SMEM(column.shape, jnp.int32),
            pltpu.SMEM(rate.shape, f32),
            pltpu.VMEM(guess.shape, f32),
            pltpu.VMEM(src.shape, f32),
            pltpu.VMEM(inv.shape, f32),
            pltpu.VMEM(cpl.shape, f32),
            pltpu.SemaphoreType.DMA((CHUNKS,)),
            pltpu.SemaphoreType.DMA((CHUNKS,)),
            pltpu.SemaphoreType.DMA((5,)),
            pltpu.SemaphoreType.DMA((2 * SIZES[1],)),
        ],
        compiler_params=pltpu.CompilerParams(vmem_limit_bytes=10 * 2**20),
        cost_estimate=pl.CostEstimate(flops=10**10, bytes_accessed=12 * 2**20, transcendentals=0),
        name="own_weights",
    )(place, *(in_hbm(array) for array in given))


def ghost_weights_kernel(batch, place, numbers_in, near, far, other_near, other_far, *refs):
    rows, pairs = BATCHES[batch]
    leads = place[1] == 0
    if batch:
        table, (bg_ref, dg_ref) = numbers_in, refs
    else:
        table, bg_ref, dg_ref, numbers, sem = refs
        copy = pltpu.make_async_copy(numbers_in.at[GROWS + SRC_TILES], numbers, sem)
        copy.start()

    def block_of(quarter, slot):
        own, other = ((near, other_near), (far, other_far))[quarter % 2]
        if quarter < 2:
            return jnp.where(leads, own[slot], other[slot])
        return jnp.where(leads, other[slot], own[slot])

    for row in range(rows):
        split_row(block_of(row // (rows // 4), row % (rows // 4)), bg_ref, row)
    if not batch:
        copy.wait()
    base = 4 * GPAIRS + 4 * sum(count for _, count in BATCHES[:batch])
    for index in range(4 * pairs):
        first = table[base + index] if batch else numbers[0, base + index].astype(jnp.int32)
        row = 2 * (index // 4) + 1 - first
        product = multiplied(block_of(index // pairs, rows // 4 + index % pairs), bg_ref, row)
        dg_ref[index // 4, pl.ds(2 * BLK * (index % 4), 2 * BLK)] = product
    if not batch:
        for index in range(8 * GPAIRS):
            table[index] = numbers[0, index].astype(jnp.int32)


SRC_TILES = GROWS // S
SENT = GROWS + SRC_TILES + 1


def ghost_weights(batch, place, numbers, *parts):
    smem, vmem = pl.BlockSpec(memory_space=pltpu.SMEM), pl.BlockSpec(memory_space=pltpu.VMEM)
    rows, pairs = BATCHES[batch]
    first = not batch
    return pl.pallas_call(
        functools.partial(ghost_weights_kernel, batch),
        out_shape=[jax.ShapeDtypeStruct((8 * GPAIRS,), jnp.int32)] * first
        + [pltpu.VMEM((rows, 2 * BLK, BLK), bf16), pltpu.VMEM((pairs, 8 * BLK, BLK), bf16)],
        in_specs=[smem, vmem if first else smem] + [vmem] * 4,
        out_specs=[smem] * first + [vmem] * 2,
        scratch_shapes=[pltpu.SMEM((S, BLK), f32), pltpu.SemaphoreType.DMA] * first,
        compiler_params=pltpu.CompilerParams(vmem_limit_bytes=8 * 2**20),
        cost_estimate=pl.CostEstimate(flops=2 * 10**9, bytes_accessed=3 * 2**20, transcendentals=0),
        name="ghost_weights",
    )(place, numbers, *parts)


BATCHES = ((2 * ((GPAIRS + 1) // 2), (GPAIRS + 1) // 2), (GROWS - 2 * ((GPAIRS + 1) // 2), GPAIRS // 2))


SIZES = tuple(rows // 4 + pairs for rows, pairs in BATCHES)


def face_copies(batch, place, inv_hbm, cpl_hbm, parts, sem):
    flipped = place[0] == 1
    rows, pairs = BATCHES[batch]
    row_base = sum(count for count, _ in BATCHES[:batch])
    index_base = 4 * sum(count for _, count in BATCHES[:batch])
    copies = []
    for side in range(2):
        quarter = 2 * place[1] + side
        for slot in range(SIZES[batch]):
            if slot < rows // 4:
                row = row_base + rows // 4 * quarter + slot
                source = inv_hbm.at[jnp.where(flipped, row, NB - 1 - row)]
            else:
                index = index_base + pairs * quarter + slot - rows // 4
                source = cpl_hbm.at[jnp.where(flipped, index, 4 * PAIRS - 1 - index)]
            copies.append(pltpu.make_async_copy(source, parts[side].at[slot], sem.at[len(copies)]))
    return copies


def face_weights_kernel(place, inv_hbm, cpl_hbm, near_ref, far_ref, sem):
    copies = face_copies(0, place, inv_hbm, cpl_hbm, (near_ref, far_ref), sem)
    for copy in copies:
        copy.start()
    for copy in copies:
        copy.wait()


def in_hbm(array):
    return pltpu.with_memory_space_constraint(array, pltpu.HBM)


def face_weights(place, inv, cpl):
    hbm, vmem = pl.BlockSpec(memory_space=pltpu.HBM), pl.BlockSpec(memory_space=pltpu.VMEM)
    return pl.pallas_call(
        face_weights_kernel,
        out_shape=(jax.ShapeDtypeStruct((SIZES[0], BLK, BLK), f32),) * 2,
        in_specs=[pl.BlockSpec(memory_space=pltpu.SMEM), hbm, hbm],
        out_specs=[vmem] * 2,
        scratch_shapes=[pltpu.SemaphoreType.DMA((2 * SIZES[0],))],
        compiler_params=pltpu.CompilerParams(vmem_limit_bytes=4 * 2**20),
        name="face_weights",
    )(place, in_hbm(inv), in_hbm(cpl))


def wavefront(stages, late):
    first = min(lo + lag for lag, lo, hi, _ in stages)
    last = max(hi + lag for lag, lo, hi, _ in stages)
    waiting = []
    for turn in range(first, last):
        ready = []
        for lag, lo, hi, item in stages:
            if lo <= turn - lag < hi:
                ready.append(item(turn - lag))
        if late:
            waiting, ready = ready, waiting
        for store in ready:
            store()
    for store in waiting:
        store()


def inverse_item(weights, u_of, src, rates, h_ref, f_ref, slot, pair):
    results = []
    for row in (2 * pair, 2 * pair + 1):
        u = u_of(row)
        right = u + step_size * (src(row) - rates * jnp.tanh(u))
        x = stacked(right)
        y = jnp.dot(jnp.concatenate([x, x], axis=1), weights(row), preferred_element_type=f32)
        results.append(y)

    def store():
        for row, y in zip((2 * pair, 2 * pair + 1), results):
            value = y[:S] + y[S:]
            f_ref[slot, row + 1] = value
            h_ref[slot, row + 1] = stacked(value)

    return store


def coupled_item(weights, cols, is_first, h_ref, f_ref, h_slot, f_slot, put, pair):
    zero = jnp.zeros((2 * S, BLK), bf16)
    top, bottom = [], []
    for slot in range(4):
        x = h_ref[h_slot, cols(4 * pair + slot)]
        if slot == 0:
            a, b = x, zero
        elif slot == 3:
            a, b = zero, x
        else:
            mine = is_first(4 * pair + slot).astype(f32).astype(bf16)
            a = x * mine
            b = x - a
        top += [a, a]
        bottom += [b, b]
    left = jnp.concatenate([jnp.concatenate(top, axis=1), jnp.concatenate(bottom, axis=1)], axis=0)
    y = jnp.dot(left, weights(pair), preferred_element_type=f32)

    def store():
        for half, row in enumerate((2 * pair, 2 * pair + 1)):
            part = y[2 * S * half : 2 * S * (half + 1)]
            put(row, f_ref[f_slot, row + 1] - (part[:S] + part[S:]))

    return store


def build_stages(ranges, bw, dw, u_first, put_last, src, rates, cols, is_first, h_ref, f_ref, late):
    stages = []
    lag = 0
    for step in range(STEPS):
        zeroth, first = 2 * step, 2 * step + 1
        inv_range, mid_range, out_range = ranges(step)
        if step == 0:
            u_of = u_first
        else:
            lag += 1 + late

            def u_of(row, slot=STEPS + step - 1):
                return f_ref[slot, row + 1]

        stages.append(
            (lag, *inv_range, functools.partial(inverse_item, bw, u_of, src, rates, h_ref, f_ref_slot(f_ref), zeroth))
        )
        lag += 2 + late

        def put_mid(row, value, slot=first):
            h_ref[slot, row + 1] = stacked(value)

        stages.append(
            (lag, *mid_range, functools.partial(coupled_item, dw, cols, is_first, h_ref, f_ref, zeroth, step, put_mid))
        )
        lag += 2 + late
        if step == STEPS - 1:
            put = put_last
        else:

            def put(row, value, slot=STEPS + step):
                f_ref[slot, row + 1] = value

        stages.append(
            (lag, *out_range, functools.partial(coupled_item, dw, cols, is_first, h_ref, f_ref, first, step, put))
        )
    return stages


class f_ref_slot:
    def __init__(self, ref):
        self.ref = ref

    def __setitem__(self, index, value):
        self.ref[index[0] // 2, index[1]] = value


def carried(step):
    base = NB - 4 * step
    return (
        (0, 2 * step, base - 4, base),
        (0, 2 * step + 1, base - 6, base - 2),
        (1, step, base - 4, base),
    )


def interior_kernel(
    cols, is_first, rate_ref, src_ref, bw_ref, dw_ref, low_ref, face_ref, out_ref, kept_h, kept_f, h_ref, f_ref
):
    for slot in range(2 * STEPS):
        h_ref[slot, 0] = jnp.zeros((2 * S, BLK), bf16)

    def u_first(row):
        return low_ref[row] if row < LOW else face_ref[NB - 1 - row]

    def put_last(row, value):
        out_ref[row] = value

    def ranges(step):
        return (0, PAIRS - 2 * step), (0, PAIRS - 2 * step - 1), (0, PAIRS - 2 * step - 2)

    wavefront(
        build_stages(
            ranges, lambda r: bw_ref[r], lambda p: dw_ref[p], u_first, put_last, lambda r: src_ref[pl.ds(r, 1)],
            rate_ref[...], lambda k: cols[k], lambda k: is_first[k], h_ref, f_ref, 1,
        ),
        1,
    )
    for step in range(STEPS):
        for buffer, slot, first, end in carried(step):
            for row in range(first, end):
                if buffer == 0:
                    kept_h[slot, row - first] = h_ref[slot, row + 1]
                else:
                    kept_f[slot, row - first] = f_ref[slot, row + 1]


def border_kernel(
    cols, is_first, table, rate_ref, src_ref, received_ref, bw_ref, dw_ref, bg0_ref, dg0_ref, bg1_ref, dg1_ref, ghost_ref,
    kept_h, kept_f,
    out_ref, h_ref, f_ref,
):
    for step in range(STEPS):
        for buffer, slot, first, end in carried(step):
            for row in range(first, end):
                if buffer == 0:
                    h_ref[slot, row + 1] = kept_h[slot, row - first]
                else:
                    f_ref[slot, row + 1] = kept_f[slot, row - first]

    def u_first(row):
        return ghost_ref[row - NB]

    def put_last(row, value):
        out_ref[NB - 1 - row] = value

    def ranges(step):
        low, count = PAIRS - 2 * step, 2 * STEPS
        return (low, low + count), (low - 1, low - 1 + count), (low - 2, low - 2 + count)

    def bw(row):
        if row < NB:
            return bw_ref[row]
        return bg0_ref[row - NB] if row - NB < BATCHES[0][0] else bg1_ref[row - NB - BATCHES[0][0]]

    def dw(pair):
        if pair < PAIRS:
            return dw_ref[pair]
        return dg0_ref[pair - PAIRS] if pair - PAIRS < BATCHES[0][1] else dg1_ref[pair - PAIRS - BATCHES[0][1]]

    def src(row):
        return src_ref[pl.ds(row, 1)] if row < NB else received_ref[GROWS + (row - NB) // S, pl.ds((row - NB) % S, 1)]

    def col(k):
        return cols[k] if k < 4 * PAIRS else table[k - 4 * PAIRS]

    def first(k):
        return is_first[k] if k < 4 * PAIRS else table[4 * GPAIRS + k - 4 * PAIRS]

    wavefront(build_stages(ranges, bw, dw, u_first, put_last, src, rate_ref[...], col, first, h_ref, f_ref, 1), 1)


SCRATCH = (
    pltpu.VMEM((2 * STEPS, WIN, 2 * S, BLK), bf16),
    pltpu.VMEM((2 * STEPS - 1, WIN, S, BLK), f32),
)


def pinned(array):
    return pltpu.with_memory_space_constraint(array, pltpu.VMEM)


def interior(cols, is_first, rates, src, bw, dw, low, face):
    vmem, smem = pl.BlockSpec(memory_space=pltpu.VMEM), pl.BlockSpec(memory_space=pltpu.SMEM)
    return pl.pallas_call(
        interior_kernel,
        out_shape=(
            jax.ShapeDtypeStruct((LOW, S, BLK), f32),
            jax.ShapeDtypeStruct((2 * STEPS, 4, 2 * S, BLK), bf16),
            jax.ShapeDtypeStruct((STEPS, 4, S, BLK), f32),
        ),
        in_specs=[smem] * 2 + [vmem] * 6,
        out_specs=[vmem] * 3,
        scratch_shapes=SCRATCH,
        compiler_params=pltpu.CompilerParams(vmem_limit_bytes=4 * 2**20),
        cost_estimate=pl.CostEstimate(flops=6 * 10**9, bytes_accessed=10 * 2**20, transcendentals=0),
        name="interior",
    )(cols, is_first, rates, src, pinned(bw), pinned(dw), low, face)


def border(cols, is_first, table, rates, src, received, weights, ghost, kept_h, kept_f):
    vmem, smem = pl.BlockSpec(memory_space=pltpu.VMEM), pl.BlockSpec(memory_space=pltpu.SMEM)
    return pl.pallas_call(
        border_kernel,
        out_shape=jax.ShapeDtypeStruct((GROWS, S, BLK), f32),
        in_specs=[smem] * 3 + [vmem] * 12,
        out_specs=vmem,
        scratch_shapes=SCRATCH,
        compiler_params=pltpu.CompilerParams(vmem_limit_bytes=4 * 2**20),
        cost_estimate=pl.CostEstimate(flops=4 * 10**9, bytes_accessed=8 * 2**20, transcendentals=0),
        name="border",
    )(
        cols, is_first, table, rates, src, received, *(pinned(array) for array in weights), ghost, kept_h, kept_f
    )


HALF = NB // 2
PACK = HALF + HALF // S


def terms_kernel(place, rate_ref, low_mid, face_mid, low, face, kept_ref, given_ref, relaxed_ref, settled_ref):
    for row in range(NB):
        relaxed_ref[row] = low_mid[row] if row < LOW else face_mid[NB - 1 - row]
        settled_ref[row] = low[row] if row < LOW else face[NB - 1 - row]
    flipped, leads = place[0] == 1, place[2] == 0
    for half, ref in ((place[1], kept_ref), (1 - place[1], given_ref)):
        for i in range(HALF):
            row = HALF * half + i
            decay = 1.0 / (1.0 + rate_ref[pl.ds(jnp.where(flipped, NB - 1 - row, row), 1)])
            carried_on = decay * relaxed_ref[row]
            term = settled_ref[row] - carried_on
            ref[i] = jnp.where(leads, carried_on + term, term)
            ref[HALF + i // S, pl.ds(i % S, 1)] = jnp.where(leads, 0.0, decay)


def terms(place, rate, low_mid, face_mid, low, face):
    vmem = pl.BlockSpec(memory_space=pltpu.VMEM)
    return pl.pallas_call(
        terms_kernel,
        out_shape=(jax.ShapeDtypeStruct((PACK, S, BLK), f32),) * 2,
        in_specs=[pl.BlockSpec(memory_space=pltpu.SMEM)] + [vmem] * 5,
        out_specs=[vmem] * 2,
        scratch_shapes=[pltpu.VMEM((NB, S, BLK), f32)] * 2,
        compiler_params=pltpu.CompilerParams(vmem_limit_bytes=2 * 2**20),
        name="terms",
    )(place, rate, low_mid, face_mid, low, face)


def assemble_kernel(place, own, swapped, low_mid, face_mid, out_ref):
    flipped, leads, core = place[0] == 1, place[2] == 0, place[1]
    for row in range(NB):
        half, i = row // HALF, row % HALF
        value = jnp.where(core == half, own[i], swapped[i])
        first = low_mid[row] if row < LOW else face_mid[NB - 1 - row]
        out_ref[jnp.where(flipped, NB - 1 - row, row)] = jnp.where(leads, first, value)


def assemble(place, own, swapped, low_mid, face_mid):
    vmem = pl.BlockSpec(memory_space=pltpu.VMEM)
    return pl.pallas_call(
        assemble_kernel,
        out_shape=jax.ShapeDtypeStruct((NB, S, BLK), f32),
        in_specs=[pl.BlockSpec(memory_space=pltpu.SMEM)] + [vmem] * 4,
        out_specs=vmem,
        compiler_params=pltpu.CompilerParams(vmem_limit_bytes=2 * 2**20),
        name="assemble",
    )(place, own, swapped, low_mid, face_mid)


def on_device(
    guess_states,
    coarse_rate,
    source,
    reaction_rate,
    inverse_blocks,
    coupling_blocks,
    column_index,
    row_offsets,
):
    tm_count = lax.axis_size("tm")
    mine, slab = lax.axis_index("tm"), lax.axis_index("space")
    core = mine & 1
    both = ("tm", "space")
    swap = [(0, 1), (1, 0)]
    across = [(2 * t + p, 2 * (t ^ 2) + 1 - p) for t in range(tm_count) for p in range(2)]

    def partner(bit):
        return [(t, t ^ (1 << bit)) for t in range(tm_count)]

    place = jnp.stack([slab, core, mine]).astype(jnp.int32)
    def fetched(near, far):
        return lax.ppermute(near, "space", swap), lax.ppermute(far, both, across)

    parts = fetched(*face_weights(place, inverse_blocks, coupling_blocks))
    cols, is_first, rates, low, face, src, sent, near_sent, far_sent, bw, dw = own_weights(
        place, row_offsets, column_index, reaction_rate,
        guess_states[0].reshape(S, NB, BLK).transpose(1, 0, 2), source.reshape(NB, BLK),
        inverse_blocks, coupling_blocks,
    )
    received = lax.ppermute(sent, "space", swap)
    parts += fetched(near_sent, far_sent)
    def shared(arrays):
        return [*arrays, *(lax.ppermute(array, "tm", partner(0)) for array in arrays)]

    near, far, low = lax.optimization_barrier((*parts[:2], low))
    batch = shared((near, far))
    held = []
    for number in range(ROUNDS):
        ghost = lax.ppermute(face, "space", swap) if number else received
        low, kept_h, kept_f = interior(cols, is_first, rates, src, bw, dw, low, face)
        if not number:
            batch[0], kept_f = lax.optimization_barrier((batch[0], kept_f))
            table, bg0, dg0 = ghost_weights(0, place, received, *batch)
            near, far, next_rate, bg0 = lax.optimization_barrier((*parts[2:], coarse_rate, bg0))
            batch = shared((near, far))
            next_rate = lax.ppermute(next_rate[0], "tm", [(t, t - 1) for t in range(1, tm_count)])
            bg1, dg1 = ghost_weights(1, place, table, *batch)
            weights = (bw, dw, bg0, dg0, bg1, dg1)
        face = border(cols, is_first, table, rates, src, received, weights, ghost, kept_h, kept_f)
        if number % (ROUNDS // 2) == ROUNDS // 2 - 1:
            held += [low, face]

    def unpacked(pack):
        return pack[HALF:].reshape(HALF, BLK), pack[:HALF]

    def packed(factor, term):
        return jnp.concatenate([term, factor.reshape(-1, S, BLK)])

    def choose(flag, left, right):
        return jnp.where(flag, left[0], right[0]), jnp.where(flag, left[1], right[1])

    def compose(earlier, later):
        return later[0] * earlier[0], later[0][:, None, :] * earlier[1] + later[1]

    kept, given = terms(place, next_rate.reshape(NB, BLK), *held)
    kept, got = unpacked(kept), unpacked(lax.ppermute(given, "tm", partner(0)))
    even = choose(core == 0, kept, got)
    odd = choose(core == 0, got, kept)
    total = compose(even, odd)
    neutral = (jnp.ones_like(total[0]), jnp.zeros_like(total[1]))
    prefix = neutral
    bits = tm_count.bit_length() - 1
    for bit in range(1, bits, 2):
        pack = packed(*total)
        three, two, one = (
            unpacked(lax.ppermute(pack, "tm", [(t, t ^ (mask << bit)) for t in range(tm_count)]))
            for mask in (3, 2, 1)
        )
        odd_place, upper = ((mine >> bit) & 1) == 1, ((mine >> (bit + 1)) & 1) == 1
        near_total = compose(choose(odd_place, one, total), choose(odd_place, total, one))
        far_total = compose(choose(odd_place, three, two), choose(odd_place, two, three))
        added = compose(choose(upper, far_total, neutral), choose(odd_place, one, neutral))
        prefix = compose(added, prefix)
        total = compose(choose(upper, far_total, near_total), choose(upper, near_total, far_total))
    end_odd = even[0][:, None, :] * prefix[1] + even[1]
    swapped = lax.ppermute(jnp.where(core == 0, end_odd, prefix[1]), "tm", partner(0))
    result = assemble(place, jnp.where(core == 0, prefix[1], end_odd), swapped, *held[:2])
    return result.transpose(1, 0, 2).reshape(1, S, NB * BLK)


def solution(mesh):
    in_specs = (
        P("tm", None, "space"),
        P("tm", "space"),
        P("space"),
        P(),
        P("space", None, None),
        P("space", None, None),
        P("space", None),
        P("space", None),
    )
    out_specs = P("tm", None, "space")
    return jax.shard_map(
        on_device, mesh=mesh, in_specs=in_specs, out_specs=out_specs, check_vma=False
    )
```
